512 devices in a mesh: grp: 16 (over y, x_hi), mem: 32 (over x_lo, z, core).
Axes of the slice: x: 4 (x_hi: 2, x_lo: 2; x = x_hi * 2 + x_lo), y: 8, z: 8, core: 2. Of those that a mesh axis runs over, the one named last changes fastest.
Arguments:
- embeddings: bfloat16 [524288, 768], P(('grp', 'mem')), may hold values from -6 to 6
- cluster_ids: int32 [524288], P(('grp', 'mem')), may hold values from 0 to 62, as said below
- valid_counts: int32 [512], P(('grp', 'mem')), may hold values from 512 to 1024
Outputs:
- best_cosine: float32 [524288], P(('grp', 'mem'))
The draws below stay inside these ranges and needn't reach their ends.
Inputs may be any that keep to these rules, and one draw needn't show every extreme that they name: `cluster_ids`: the rows form a cycle (row 524287 is followed by row 0); every cluster is one contiguous run of rows on this cycle.
All inputs are finite; a program needn't handle non-finite values.
Results may differ from the reference program's by a relative error of at most 0.0003.
Values may be sent and summed in bfloat16 or wider, within the bound.
A program may use at most 64 MiB of HBM per device.

```python
import jax
import jax.numpy as jnp
from jax import lax

D = 768
ROW_DEV = 1024
ROUNDS = 3
BLOCKS = 512
ROWS = 524288
CLUSTERS = 64
N_GRP = 16
N_MEM = 32


def draw_cluster_ids(key, part):
    key = jax.random.fold_in(key, 7)
    total = ROWS
    cuts = jax.random.permutation(key, total - ROW_DEV - 1)[:CLUSTERS - 1].astype(jnp.int32) + 1
    positions = jnp.arange(total, dtype=jnp.int32)

    def count_cuts(carry, cut):
        return (carry + (positions >= cut).astype(jnp.int32), None)
    labels, unused = lax.scan(count_cuts, jnp.zeros((total,), jnp.int32), cuts)
    wrapped = (labels == CLUSTERS - 1) | (positions >= total - ROW_DEV)
    return jnp.where(wrapped, 0, labels).astype(jnp.int32)


def set_ends(array, key, low, high):
    longest = array.shape.index(max(array.shape))
    spots = []
    for shift in (0, 1):
        where = [jax.random.randint(jax.random.fold_in(key, axis), (), 0, length) for axis, length in enumerate(array.shape)]
        where[longest] = (where[longest] + shift) % array.shape[longest]
        spots.append(tuple(where))
    return array.at[spots[0]].set(low).at[spots[1]].set(high)


def level_of(rng, dims, cuts, smallest, largest):
    gain, own = 1.0, jax.random.fold_in(rng, 6)
    for dim, shards_of in cuts:
        steps = jnp.exp(jax.random.uniform(jax.random.fold_in(own, dim), (shards_of,), jnp.float32, smallest / len(cuts), largest / len(cuts)))
        gain = gain * jnp.repeat(steps, dims[dim] // shards_of).reshape([-1 if axis == dim else 1 for axis in range(len(dims))])
    return gain


def scatter_about(own_key, shape, scale, most, pieces=(), held_as=jnp.bfloat16):
    drawn = jax.random.normal(own_key, shape, jnp.float32) * scale
    if len(pieces) > 0:
        drawn = level_of(own_key, shape, pieces, -0.22, 0.18) * drawn
    return jnp.clip(drawn, min=-most, max=most).astype(held_as)


def setup_inputs(seed: int = 0) -> dict:
    arg_keys = jax.random.split(jax.random.key(seed), 4)
    return {
        "embeddings": scatter_about(arg_keys[0], (ROWS, D), 1.0, 6.0, ((0, 512),)),
        "cluster_ids": draw_cluster_ids(jax.random.fold_in(arg_keys[3], 71), 0),
        "valid_counts": set_ends(jax.random.randint(arg_keys[2], (BLOCKS,), ROW_DEV // 2, ROW_DEV + 1), jax.random.fold_in(arg_keys[2], 1), ROW_DEV // 2, ROW_DEV).astype(jnp.int32),
    }


EPS = 1e-06

def pair_maxima(left, left_scale, left_ids, left_valid, right, right_scale, right_ids, right_valid):
    dots = jnp.dot(left, right.T, preferred_element_type=jnp.float32)
    cosine = dots * left_scale[:, None] * right_scale[None, :]
    same = left_ids[:, None] == right_ids[None, :]
    row_best = lax.optimization_barrier(jnp.max(jnp.where(same & right_valid[None, :], cosine, -2.0), axis=1))
    col_best = lax.optimization_barrier(jnp.max(jnp.where(same & left_valid[:, None], cosine, -2.0), axis=0))
    return (row_best, col_best)

def reference(embeddings, cluster_ids, valid_counts):
    blocks = N_GRP * N_MEM
    emb = embeddings.reshape(blocks, ROW_DEV, D)
    ids = cluster_ids.reshape(blocks, ROW_DEV)
    positions = jnp.arange(ROW_DEV, dtype=jnp.int32)
    valid = positions[None, :] < valid_counts[:, None]
    scale = lax.rsqrt(lax.optimization_barrier(jnp.sum(jnp.square(emb.astype(jnp.float32)), axis=2)) + EPS)
    not_self = positions[:, None] != positions[None, :]

    def own_block(items):
        block, block_scale, block_ids, block_valid = items
        dots = jnp.dot(block, block.T, preferred_element_type=jnp.float32)
        cosine = dots * block_scale[:, None] * block_scale[None, :]
        keep = (block_ids[:, None] == block_ids[None, :]) & block_valid[None, :] & not_self
        return lax.optimization_barrier(jnp.max(jnp.where(keep, cosine, -2.0), axis=1))
    best = lax.map(own_block, (emb, scale, ids, valid))
    for offset in range(1, ROUNDS + 1):
        items = (emb, scale, ids, valid, jnp.roll(emb, -offset, axis=0), jnp.roll(scale, -offset, axis=0), jnp.roll(ids, -offset, axis=0), jnp.roll(valid, -offset, axis=0))
        row_best, col_best = lax.map(lambda t: pair_maxima(*t), items)
        best = jnp.maximum(best, row_best)
        best = jnp.maximum(best, jnp.roll(col_best, offset, axis=0))
    return best.reshape(ROWS)
```

```python
import functools

import jax
import jax.numpy as jnp
from jax import lax
from jax.experimental import pallas as pl
from jax.experimental.pallas import tpu as pltpu
from jax.sharding import PartitionSpec as P

MESH = pl.DeviceIdType.MESH
EPS = 1e-06
LOW = -3.0e38
XS = 4
CH = 256

A, B, LO, UP = 0, 1, 2, 3


def kernel(
    blocks, emb, ids, count, out,
    rows, relay, cmeta, rmeta, racc, cacc, vec, got,
    own_sem, sib_sem, up_send, up_recv, lo_send, lo_recv, via_send, via_recv, fwd_send,
    meta_send, meta_recv, vec_send, vec_recv,
):
    n, d = emb.shape
    chunks = n // CH
    half = chunks // 2
    mem = lax.axis_size("mem")
    zs = mem // (2 * 2)
    b = lax.axis_index("grp") * mem + lax.axis_index("mem")

    def device(i):
        i = lax.rem(i + blocks, blocks)
        return (i // mem, lax.rem(i, mem))

    def place(i):
        c = lax.rem(i + blocks, blocks) // 2
        return lax.rem(c // zs, XS), lax.rem(c, zs)

    core = lax.rem(b, 2)
    x, z = place(b)
    x_below, _ = place(b - 2)
    even, even_below = lax.rem(x, 2) == 0, lax.rem(x_below, 2) == 0
    first, second = core == 0, core == 1
    has_up = jnp.logical_or(first, even)
    has_lo = jnp.logical_or(first, jnp.logical_not(even_below))
    send_down = jnp.logical_or(first, even_below)
    send_up = jnp.logical_or(second, jnp.logical_not(even))
    sibling = b + 1 - 2 * core
    down, up = b - 2, b + 3 - 2 * core
    above, below = b + 2, b - 1 - 2 * core
    step = 2 * zs

    def flip(i):
        return i + step - 2 * step * lax.rem(place(i)[0], 2)

    via_down = jnp.logical_and(second, even_below)
    via_up = jnp.logical_and(first, jnp.logical_not(even))
    uses_via = jnp.logical_or(via_down, via_up)
    ring_up = jnp.where(x == XS - 1, b - (XS - 1) * step, b + step)
    ring_down = jnp.where(x == 0, b + (XS - 1) * step, b - step)
    last = z == zs - 1
    via = jnp.where(jnp.logical_and(first, last), ring_up, flip(b))
    is_relay = jnp.where(
        first, even, jnp.logical_or(jnp.logical_and(jnp.logical_not(even), z > 0), jnp.logical_and(even, z == 0))
    )
    relay_from = jnp.where(jnp.logical_and(first, last), ring_down, flip(b))
    relay_to = jnp.where(first, relay_from + 3, relay_from - 2)
    split_up = jnp.logical_and(second, has_up)
    split_lo = jnp.logical_and(second, has_lo)
    up_relay = flip(b + 2)
    lo_src = b - 3
    lo_x, lo_z = place(lo_src)
    lo_relay = jnp.where(
        lo_z == zs - 1, jnp.where(lo_x == XS - 1, lo_src - (XS - 1) * step, lo_src + step), flip(lo_src)
    )

    mine = pl.ds(pl.multiple_of(core * n, n), n)
    own = pltpu.make_async_copy(emb, rows.at[mine], own_sem)
    own.start()

    barrier = pltpu.get_barrier_semaphore()

    def greet(i):
        pl.semaphore_signal(barrier, inc=1, device_id=device(i), device_id_type=MESH)

    for i in (sibling, down, up, above, below):
        greet(i)
    pl.when(is_relay)(lambda: greet(relay_from))
    pl.when(split_up)(lambda: greet(up_relay))
    pl.when(split_lo)(lambda: greet(lo_relay))
    pl.semaphore_wait(barrier, 5 + uses_via.astype(jnp.int32) + is_relay.astype(jnp.int32))

    def copy(src, dst, send, recv, to):
        return pltpu.make_async_remote_copy(
            src_ref=src, dst_ref=dst, send_sem=send, recv_sem=recv, device_id=device(to), device_id_type=MESH
        )

    def part(slot, k):
        return pl.ds(slot * n + k * CH, CH)

    def emb_part(k):
        return emb.at[pl.ds(k * CH, CH)]

    swap = copy(emb, rows.at[mine], sib_sem.at[0], sib_sem.at[1], sibling)
    swap.start()
    downs = [copy(emb_part(k), rows.at[part(UP, k)], up_send.at[k], up_recv.at[k], down) for k in range(chunks)]
    ups = [copy(emb_part(k), rows.at[part(LO, k)], lo_send.at[k], lo_recv.at[k], up) for k in range(chunks)]
    vias = [
        copy(emb_part(half + k), relay.at[pl.ds(k * CH, CH)], via_send.at[k], via_recv.at[k], via) for k in range(half)
    ]
    fwd_up = [
        copy(relay.at[pl.ds(k * CH, CH)], rows.at[part(LO, half + k)], fwd_send.at[k], lo_recv.at[half + k], relay_to)
        for k in range(half)
    ]
    fwd_down = [
        copy(relay.at[pl.ds(k * CH, CH)], rows.at[part(UP, half + k)], fwd_send.at[k], up_recv.at[half + k], relay_to)
        for k in range(half)
    ]
    whole_down = jnp.logical_and(send_down, first)
    whole_up = jnp.logical_and(send_up, second)

    for k in range(half):
        pl.when(uses_via)(vias[k].start)
    for k in range(chunks):
        pl.when(send_down if k < half else whole_down)(downs[k].start)
        pl.when(send_up if k < half else whole_up)(ups[k].start)

    own.wait()
    cacc[...] = jnp.full(cacc.shape, LOW, jnp.float32)
    racc[...] = jnp.full(racc.shape, LOW, jnp.float32)
    lanes = lax.broadcasted_iota(jnp.int32, (1, n), 1)
    own_ids = ids[...].astype(jnp.float32)
    valid_ids = jnp.where(lanes < count[0], own_ids, -1.0)
    cmeta[1:2, mine] = own_ids
    cmeta[2:3, mine] = valid_ids

    def squares(t, _):
        at = pl.ds(pl.multiple_of(core * n + t * 128, 128), 128)
        block = rows[at, :].astype(jnp.float32)
        scale = lax.rsqrt(jnp.sum(block * block, axis=1, keepdims=True) + EPS)
        wide = jnp.broadcast_to(scale, (128, 128))
        cmeta[0:1, at] = wide.T[0:1]
        return 0

    lax.fori_loop(0, n // 128, squares, 0)

    def spread(slot):
        def group(t, _):
            at = pl.ds(pl.multiple_of(slot * n + t * 128, 128), 128)
            for j in range(3):
                rmeta[j, at, :] = jnp.broadcast_to(cmeta[j : j + 1, at], (128, 128)).T
            return 0

        lax.fori_loop(0, n // 128, group, 0)

    def meta(slot):
        return cmeta.at[:, pl.ds(slot * n, n)]

    meta_sib = copy(cmeta.at[:, mine], cmeta.at[:, mine], meta_send.at[0], meta_recv.at[0], sibling)
    meta_down = copy(cmeta.at[:, mine], meta(UP), meta_send.at[1], meta_recv.at[1], down)
    meta_up = copy(cmeta.at[:, mine], meta(LO), meta_send.at[2], meta_recv.at[2], up)
    meta_sib.start()
    pl.when(send_down)(meta_down.start)
    pl.when(send_up)(meta_up.start)
    spread(core)

    def cosines(row, col, masked_diagonal):
        return lax.dot_general(
            rows[pl.ds(row, CH), :], rows[pl.ds(col, CH), :], (((1,), (1,)), ((), ())),
            preferred_element_type=jnp.float32,
        )

    def fold(values):
        return jnp.max(values.reshape(CH // 8, 8, 128), axis=0)

    def run(col, row, tiles):
        col = pl.multiple_of(col, CH)

        def tile(t, best):
            at = pl.multiple_of(row + t * CH, CH)
            dots = cosines(at, col, False)
            at = pl.ds(at, CH)
            scale, own_id, own_valid = rmeta[0, at, :], rmeta[1, at, :], rmeta[2, at, :]
            row_best = racc[at, :]
            out_best = []
            for h in range(CH // 128):
                lane = pl.ds(pl.multiple_of(col + h * 128, 128), 128)
                dot = dots[:, h * 128 : (h + 1) * 128]
                row_best = jnp.maximum(
                    row_best, jnp.where(own_id == cmeta[2:3, lane], dot * cmeta[0:1, lane], LOW)
                )
                out_best.append(
                    jnp.maximum(best[h], fold(jnp.where(own_valid == cmeta[1:2, lane], dot * scale, LOW)))
                )
            racc[at, :] = row_best
            return tuple(out_best)

        def lanes_of(h):
            return pl.ds(pl.multiple_of(col + h * 128, 128), 128)

        start = tuple(cacc[:, lanes_of(h)] for h in range(CH // 128))
        end = lax.fori_loop(0, tiles, tile, start)
        for h in range(CH // 128):
            cacc[:, lanes_of(h)] = end[h]

    def run_self(col, row):
        col = pl.multiple_of(col, CH)

        def tile(t, best):
            first_row = pl.multiple_of(row + t * CH, CH)
            dots = cosines(first_row, col, True)
            at = pl.ds(first_row, CH)
            scale, own_valid = rmeta[0, at, :], rmeta[2, at, :]
            apart = lax.broadcasted_iota(jnp.int32, (CH, 128), 1) - lax.broadcasted_iota(jnp.int32, (CH, 128), 0)
            out_best = []
            for h in range(CH // 128):
                lane = pl.ds(pl.multiple_of(col + h * 128, 128), 128)
                dot = dots[:, h * 128 : (h + 1) * 128]
                keep = jnp.logical_and(own_valid == cmeta[1:2, lane], apart != first_row - col - h * 128)
                out_best.append(jnp.maximum(best[h], fold(jnp.where(keep, dot * scale, LOW))))
            return tuple(out_best)

        start = tuple(jnp.full((8, 128), LOW, jnp.float32) for _ in range(CH // 128))
        end = lax.fori_loop(0, n // CH, tile, start)
        for h in range(CH // 128):
            cacc[:, pl.ds(pl.multiple_of(col + h * 128, 128), 128)] = end[h]

    def own_chunk(k, _):
        run_self(core * n + k * CH, core * n)
        return 0

    lax.fori_loop(0, chunks, own_chunk, 0)

    meta_sib.wait_recv()
    theirs = pl.ds(pl.multiple_of(n - core * n, n), n)
    copy(emb, rows.at[theirs], sib_sem.at[0], sib_sem.at[1], sibling).wait_recv()
    spread(1 - core)

    def sibling_chunk(k, _):
        run(B * n + k * CH, A * n, core * chunks)
        return 0

    lax.fori_loop(0, chunks, sibling_chunk, 0)

    pl.when(has_up)(meta_down.wait_recv)
    pl.when(has_up)(lambda: spread(UP))
    pl.when(has_lo)(meta_up.wait_recv)
    pl.when(has_lo)(lambda: spread(LO))

    zero = core * 0
    for k in range(chunks):
        if k < half:

            @pl.when(is_relay)
            def _():
                vias[k].wait_recv()

            pl.when(jnp.logical_and(is_relay, first))(fwd_up[k].start)
            pl.when(jnp.logical_and(is_relay, second))(fwd_down[k].start)
        pl.when(has_up)(downs[k].wait_recv)
        pl.when(has_lo)(ups[k].wait_recv)
        run(UP * n + k * CH, A * n, jnp.where(first, 2 * chunks + k, jnp.where(has_up, 2 * chunks, zero)))
        run(LO * n + k * CH, UP * n, jnp.where(first, k + 1, zero))
        run(LO * n + k * CH, B * n, jnp.where(even_below, zero, chunks))

    def finish(slot):
        def group(t, _):
            at = pl.ds(pl.multiple_of(slot * n + t * 128, 128), 128)
            best = jnp.maximum(
                jnp.max(racc[at, :].T, axis=0, keepdims=True), jnp.max(cacc[:, at], axis=0, keepdims=True)
            )
            vec[slot, pl.ds(t, 1), :] = best * cmeta[0:1, at]
            return 0

        lax.fori_loop(0, n // 128, group, 0)

    send_vec_up = copy(vec.at[UP], got.at[1], vec_send.at[1], vec_recv.at[1], above)
    send_vec_lo = copy(vec.at[LO], got.at[2], vec_send.at[2], vec_recv.at[2], below)
    send_vec_sib = copy(vec.at[1 - core], got.at[0], vec_send.at[0], vec_recv.at[0], sibling)

    @pl.when(has_up)
    def _():
        finish(UP)
        send_vec_up.start()

    @pl.when(has_lo)
    def _():
        finish(LO)
        send_vec_lo.start()

    finish(1 - core)
    send_vec_sib.start()
    finish(core)
    best = jnp.maximum(vec[core], -2.0)
    got_down, got_up = send_down, send_up
    send_vec_sib.wait_recv()
    best = jnp.maximum(best, got[0])
    out[...] = best

    @pl.when(got_down)
    def _():
        send_vec_up.wait_recv()
        out[...] = jnp.maximum(out[...], got[1])

    @pl.when(got_up)
    def _():
        send_vec_lo.wait_recv()
        out[...] = jnp.maximum(out[...], got[2])

    swap.wait_send()
    meta_sib.wait_send()
    send_vec_sib.wait_send()
    pl.when(send_down)(meta_down.wait_send)
    pl.when(send_up)(meta_up.wait_send)
    pl.when(has_up)(send_vec_up.wait_send)
    pl.when(has_lo)(send_vec_lo.wait_send)
    for k in range(half):
        pl.when(uses_via)(vias[k].wait_send)
        pl.when(is_relay)(fwd_up[k].wait_send)
    for k in range(chunks):
        pl.when(send_down if k < half else whole_down)(downs[k].wait_send)
        pl.when(send_up if k < half else whole_up)(ups[k].wait_send)


def shards(blocks, embeddings, cluster_ids, valid_counts):
    n, d = embeddings.shape
    chunks = n // CH
    dma = pltpu.SemaphoreType.DMA
    best = pl.pallas_call(
        functools.partial(kernel, blocks),
        out_shape=jax.ShapeDtypeStruct((n // 128, 128), jnp.float32),
        in_specs=[
            pl.BlockSpec(memory_space=pl.ANY),
            pl.BlockSpec(memory_space=pltpu.VMEM),
            pl.BlockSpec(memory_space=pltpu.SMEM),
        ],
        out_specs=pl.BlockSpec(memory_space=pltpu.VMEM),
        scratch_shapes=[
            pltpu.VMEM((4 * n, d), jnp.bfloat16),
            pltpu.VMEM((n // 2, d), jnp.bfloat16),
            pltpu.VMEM((8, 4 * n), jnp.float32),
            pltpu.VMEM((3, 4 * n, 128), jnp.float32),
            pltpu.VMEM((4 * n, 128), jnp.float32),
            pltpu.VMEM((8, 4 * n), jnp.float32),
            pltpu.VMEM((4, n // 128, 128), jnp.float32),
            pltpu.VMEM((3, n // 128, 128), jnp.float32),
            dma(()), dma((2,)),
            dma((chunks,)), dma((chunks,)), dma((chunks,)), dma((chunks,)),
            dma((chunks // 2,)), dma((chunks // 2,)), dma((chunks // 2,)),
            dma((3,)), dma((3,)), dma((3,)), dma((3,)),
        ],
        compiler_params=pltpu.CompilerParams(
            collective_id=0, has_side_effects=True, vmem_limit_bytes=56 * 2**20
        ),
        name="neighbour_cosines",
    )(embeddings, cluster_ids.reshape(1, n), valid_counts)
    return best.reshape(n)


def solution(mesh):
    placed = (P(("grp", "mem"), None), P(("grp", "mem")), P(("grp", "mem")))
    return jax.shard_map(
        functools.partial(shards, mesh.size),
        mesh=mesh, in_specs=placed, out_specs=P(("grp", "mem")), check_vma=False,
    )
```

```python
import functools

import jax
import jax.numpy as jnp
from jax import lax
from jax.experimental import pallas as pl
from jax.experimental.pallas import tpu as pltpu
from jax.sharding import PartitionSpec as P

MESH = pl.DeviceIdType.MESH
EPS = 1e-06
LOW = -3.0e38
XS = 4
CH = 256

A, B, LO, UP = 0, 1, 2, 3


def kernel(
    blocks, emb, ids, count, out,
    rows, relay, cmeta, rmeta, racc, cacc, vec, got,
    own_sem, sib_sem, up_send, up_recv, lo_send, lo_recv, via_send, via_recv, fwd_send,
    meta_send, meta_recv, vec_send, vec_recv,
):
    n, d = emb.shape
    chunks = n // CH
    half = chunks // 2
    mem = lax.axis_size("mem")
    zs = mem // (2 * 2)
    b = lax.axis_index("grp") * mem + lax.axis_index("mem")

    def device(i):
        i = lax.rem(i + blocks, blocks)
        return (i // mem, lax.rem(i, mem))

    def place(i):
        c = lax.rem(i + blocks, blocks) // 2
        return lax.rem(c // zs, XS), lax.rem(c, zs)

    core = lax.rem(b, 2)
    first, second = core == 0, core == 1
    step = 2 * zs

    def goes_down(i):
        x, z = place(i)
        return (lax.rem(x, 2) == 0) != (z == 0)

    def next_x(i):
        return jnp.where(place(i)[0] == XS - 1, i - (XS - 1) * step, i + step)

    def last_x(i):
        return jnp.where(place(i)[0] == 0, i + (XS - 1) * step, i - step)

    def relay_down(i):
        return jnp.where(place(i)[1] == 0, last_x(i), next_x(i))

    def relay_up(i):
        return jnp.where(place(i)[1] == zs - 1, next_x(i), last_x(i))

    up_down, lo_down = goes_down(b), goes_down(b - 2)
    has_up = jnp.logical_or(first, up_down)
    has_lo = jnp.logical_or(first, jnp.logical_not(lo_down))
    send_down = jnp.logical_or(first, lo_down)
    send_up = jnp.logical_or(second, jnp.logical_not(up_down))
    sibling = b + 1 - 2 * core
    down, up = b - 2, b + 3 - 2 * core
    above, below = b + 2, b - 1 - 2 * core

    via_down = jnp.logical_and(second, lo_down)
    via_up = jnp.logical_and(first, jnp.logical_not(up_down))
    uses_via = jnp.logical_or(via_down, via_up)
    via = jnp.where(first, relay_up(b), relay_down(b))
    z = place(b)[1]
    relay_from = jnp.where(
        jnp.where(first, z == zs - 1, z != 0), last_x(b), next_x(b)
    )
    is_relay = jnp.where(first, jnp.logical_not(goes_down(relay_from)), goes_down(relay_from - 2))
    relay_to = jnp.where(first, relay_from + 3, relay_from - 2)
    split_up = jnp.logical_and(second, has_up)
    split_lo = jnp.logical_and(second, has_lo)
    up_relay, lo_relay = relay_down(b + 2), relay_up(b - 3)

    mine = pl.ds(pl.multiple_of(core * n, n), n)
    own = pltpu.make_async_copy(emb, rows.at[mine], own_sem)
    own.start()

    barrier = pltpu.get_barrier_semaphore()

    def greet(i):
        pl.semaphore_signal(barrier, inc=1, device_id=device(i), device_id_type=MESH)

    for i in (sibling, down, up, above, below):
        greet(i)
    pl.when(is_relay)(lambda: greet(relay_from))
    pl.when(split_up)(lambda: greet(up_relay))
    pl.when(split_lo)(lambda: greet(lo_relay))
    pl.semaphore_wait(barrier, 5 + uses_via.astype(jnp.int32) + is_relay.astype(jnp.int32))

    def copy(src, dst, send, recv, to):
        return pltpu.make_async_remote_copy(
            src_ref=src, dst_ref=dst, send_sem=send, recv_sem=recv, device_id=device(to), device_id_type=MESH
        )

    def part(slot, k):
        return pl.ds(pl.multiple_of(slot * n + k * CH, CH), CH)

    def emb_part(k):
        return emb.at[pl.ds(pl.multiple_of(k * CH, CH), CH)]

    swap = copy(emb, rows.at[mine], sib_sem.at[0], sib_sem.at[1], sibling)
    swap.start()
    downs = [copy(emb_part(k), rows.at[part(UP, k)], up_send.at[k], up_recv.at[k], down) for k in range(chunks)]
    ups = [copy(emb_part(k), rows.at[part(LO, k)], lo_send.at[k], lo_recv.at[k], up) for k in range(chunks)]
    vias = [
        copy(emb_part(half + k), relay.at[pl.ds(k * CH, CH)], via_send.at[k], via_recv.at[k], via) for k in range(half)
    ]
    fwd_up = [
        copy(relay.at[pl.ds(k * CH, CH)], rows.at[part(LO, half + k)], fwd_send.at[k], lo_recv.at[half + k], relay_to)
        for k in range(half)
    ]
    fwd_down = [
        copy(relay.at[pl.ds(k * CH, CH)], rows.at[part(UP, half + k)], fwd_send.at[k], up_recv.at[half + k], relay_to)
        for k in range(half)
    ]
    def send(k):
        if k < half:
            pl.when(uses_via)(vias[k].start)
        pl.when(first)(downs[k].start)
        pl.when(second)(ups[k].start)
        if k < half:
            pl.when(via_down)(downs[k].start)
            pl.when(via_up)(ups[k].start)

    send(0)

    def forward(k):
        pl.when(is_relay)(vias[k].wait_recv)
        pl.when(jnp.logical_and(is_relay, first))(fwd_up[k].start)
        pl.when(jnp.logical_and(is_relay, second))(fwd_down[k].start)

    own.wait()
    cacc[...] = jnp.full(cacc.shape, LOW, jnp.float32)
    racc[...] = jnp.full(racc.shape, LOW, jnp.float32)
    lanes = lax.broadcasted_iota(jnp.int32, (1, n), 1)
    own_ids = ids[...].astype(jnp.float32)
    valid_ids = jnp.where(lanes < count[0], own_ids, -1.0)
    cmeta[1:2, mine] = own_ids
    cmeta[2:3, mine] = valid_ids

    def squares(t, _):
        at = pl.ds(pl.multiple_of(core * n + t * 128, 128), 128)
        block = rows[at, :].astype(jnp.float32)
        scale = lax.rsqrt(jnp.sum(block * block, axis=1, keepdims=True) + EPS)
        wide = jnp.broadcast_to(scale, (128, 128))
        cmeta[0:1, at] = wide.T[0:1]
        return 0

    lax.fori_loop(0, n // 128, squares, 0)

    def spread(slot):
        def group(t, _):
            at = pl.ds(pl.multiple_of(slot * n + t * 128, 128), 128)
            for j in range(3):
                rmeta[j, at, :] = jnp.broadcast_to(cmeta[j : j + 1, at], (128, 128)).T
            return 0

        lax.fori_loop(0, n // 128, group, 0)

    def meta(slot):
        return cmeta.at[:, pl.ds(slot * n, n)]

    meta_sib = copy(cmeta.at[:, mine], cmeta.at[:, mine], meta_send.at[0], meta_recv.at[0], sibling)
    meta_down = copy(cmeta.at[:, mine], meta(UP), meta_send.at[1], meta_recv.at[1], down)
    meta_up = copy(cmeta.at[:, mine], meta(LO), meta_send.at[2], meta_recv.at[2], up)
    meta_sib.start()
    pl.when(send_down)(meta_down.start)
    pl.when(send_up)(meta_up.start)
    for k in range(1, chunks):
        send(k)
    spread(core)

    def dots(row, col):
        return lax.dot_general(
            rows[pl.ds(row, n), :], rows[pl.ds(col, CH), :], (((1,), (1,)), ((), ())),
            preferred_element_type=jnp.float32,
        )

    def fold(values):
        return jnp.max(values.reshape(n // 8, 8, 128), axis=0)

    def lanes_of(col, h):
        return pl.ds(pl.multiple_of(col + h * 128, 128), 128)

    def pair(col, row):
        col, row = pl.multiple_of(col, CH), pl.multiple_of(row, n)
        dot = dots(row, col)
        at = pl.ds(row, n)
        scale, own_id, own_valid = rmeta[0, at, :], rmeta[1, at, :], rmeta[2, at, :]
        row_best = racc[at, :]
        for h in range(CH // 128):
            lane = lanes_of(col, h)
            d = dot[:, h * 128 : (h + 1) * 128]
            row_best = jnp.maximum(row_best, jnp.where(own_id == cmeta[2:3, lane], d * cmeta[0:1, lane], LOW))
            col_best = fold(jnp.where(own_valid == cmeta[1:2, lane], d * scale, LOW))
            cacc[:, lane] = jnp.maximum(cacc[:, lane], col_best)
        racc[at, :] = row_best

    def own_chunk(k, _):
        row = pl.multiple_of(core * n, n)
        col = pl.multiple_of(row + k * CH, CH)
        dot = dots(row, col)
        at = pl.ds(row, n)
        scale, own_valid = rmeta[0, at, :], rmeta[2, at, :]
        apart = lax.broadcasted_iota(jnp.int32, (n, 128), 0) - lax.broadcasted_iota(jnp.int32, (n, 128), 1)
        for h in range(CH // 128):
            lane = lanes_of(col, h)
            d = dot[:, h * 128 : (h + 1) * 128]
            keep = jnp.logical_and(own_valid == cmeta[1:2, lane], apart != k * CH + h * 128)
            cacc[:, lane] = fold(jnp.where(keep, d * scale, LOW))
        return 0

    lax.fori_loop(0, chunks, own_chunk, 0)

    meta_sib.wait_recv()
    theirs = pl.ds(pl.multiple_of(n - core * n, n), n)
    copy(emb, rows.at[theirs], sib_sem.at[0], sib_sem.at[1], sibling).wait_recv()
    spread(1 - core)

    for k in range(half):
        forward(k)

    end = chunks + 1

    def stage(e, _):
        arrival = jnp.logical_and(e >= 1, e < end)
        k = jnp.where(first, e - 1, lax.rem(e - 1 + chunks, 2) * half + (e - 1 + chunks) // 2 - half)
        k = jnp.clip(k, 0, chunks - 1)

        @pl.when(e == 1)
        def _():
            pl.when(has_up)(meta_down.wait_recv)
            pl.when(has_up)(lambda: spread(UP))
            pl.when(has_lo)(meta_up.wait_recv)
            pl.when(has_lo)(lambda: spread(LO))

        @pl.when(jnp.logical_and(arrival, has_up))
        def _():
            copy(emb_part(k), rows.at[part(UP, k)], up_send.at[k], up_recv.at[k], down).wait_recv()

        @pl.when(jnp.logical_and(arrival, has_lo))
        def _():
            copy(emb_part(k), rows.at[part(LO, k)], lo_send.at[k], lo_recv.at[k], up).wait_recv()

        def unit(j, _):
            slot = jnp.where(j < 2, UP, LO)
            col = jnp.where(arrival, slot * n + k * CH, jnp.where(e == 0, B, LO) * n + j * CH)
            row = jnp.where(arrival, jnp.where(j == 0, A, B), jnp.where(e == 0, A, UP))
            wanted = jnp.where(
                arrival,
                jnp.where(j < 2, has_up, jnp.logical_and(j == 2, jnp.logical_not(lo_down))).astype(jnp.int32),
                jnp.where(e == 0, second, first).astype(jnp.int32),
            )
            pl.when(wanted == 1)(lambda: pair(col, row * n))
            return 0

        lax.fori_loop(0, chunks, unit, 0)
        return 0

    lax.fori_loop(0, end + 1, stage, 0)

    def finish(slot):
        for t in range(n // 128):
            at = pl.ds(pl.multiple_of(slot * n + t * 128, 128), 128)
            best = jnp.maximum(
                jnp.max(racc[at, :].T, axis=0, keepdims=True), jnp.max(cacc[:, at], axis=0, keepdims=True)
            )
            vec[slot, t : t + 1, :] = best * cmeta[0:1, at]

    send_vec_up = copy(vec.at[UP], got.at[1], vec_send.at[1], vec_recv.at[1], above)
    send_vec_lo = copy(vec.at[LO], got.at[2], vec_send.at[2], vec_recv.at[2], below)
    send_vec_sib = copy(vec.at[1 - core], got.at[0], vec_send.at[0], vec_recv.at[0], sibling)

    @pl.when(has_up)
    def _():
        finish(UP)
        send_vec_up.start()

    @pl.when(has_lo)
    def _():
        finish(LO)
        send_vec_lo.start()

    finish(1 - core)
    send_vec_sib.start()
    finish(core)
    best = jnp.maximum(vec[core], -2.0)
    got_down, got_up = send_down, send_up
    send_vec_sib.wait_recv()
    best = jnp.maximum(best, got[0])
    out[...] = best

    @pl.when(got_down)
    def _():
        send_vec_up.wait_recv()
        out[...] = jnp.maximum(out[...], got[1])

    @pl.when(got_up)
    def _():
        send_vec_lo.wait_recv()
        out[...] = jnp.maximum(out[...], got[2])

    swap.wait_send()
    meta_sib.wait_send()
    send_vec_sib.wait_send()
    pl.when(send_down)(meta_down.wait_send)
    pl.when(send_up)(meta_up.wait_send)
    pl.when(has_up)(send_vec_up.wait_send)
    pl.when(has_lo)(send_vec_lo.wait_send)
    for k in range(half):
        pl.when(uses_via)(vias[k].wait_send)
        pl.when(is_relay)(fwd_up[k].wait_send)
    for k in range(chunks):
        pl.when(send_down if k < half else first)(downs[k].wait_send)
        pl.when(send_up if k < half else second)(ups[k].wait_send)


def shards(blocks, embeddings, cluster_ids, valid_counts):
    n, d = embeddings.shape
    chunks = n // CH
    dma = pltpu.SemaphoreType.DMA
    best = pl.pallas_call(
        functools.partial(kernel, blocks),
        out_shape=jax.ShapeDtypeStruct((n // 128, 128), jnp.float32),
        in_specs=[
            pl.BlockSpec(memory_space=pl.ANY),
            pl.BlockSpec(memory_space=pltpu.VMEM),
            pl.BlockSpec(memory_space=pltpu.SMEM),
        ],
        out_specs=pl.BlockSpec(memory_space=pltpu.VMEM),
        scratch_shapes=[
            pltpu.VMEM((4 * n, d), jnp.bfloat16),
            pltpu.VMEM((n // 2, d), jnp.bfloat16),
            pltpu.VMEM((8, 4 * n), jnp.float32),
            pltpu.VMEM((3, 4 * n, 128), jnp.float32),
            pltpu.VMEM((4 * n, 128), jnp.float32),
            pltpu.VMEM((8, 4 * n), jnp.float32),
            pltpu.VMEM((4, n // 128, 128), jnp.float32),
            pltpu.VMEM((3, n // 128, 128), jnp.float32),
            dma(()), dma((2,)),
            dma((chunks,)), dma((chunks,)), dma((chunks,)), dma((chunks,)),
            dma((chunks // 2,)), dma((chunks // 2,)), dma((chunks // 2,)),
            dma((3,)), dma((3,)), dma((3,)), dma((3,)),
        ],
        compiler_params=pltpu.CompilerParams(
            collective_id=0, has_side_effects=True, vmem_limit_bytes=56 * 2**20
        ),
        name="neighbour_cosines",
    )(embeddings, cluster_ids.reshape(1, n), valid_counts)
    return best.reshape(n)


def solution(mesh):
    placed = (P(("grp", "mem"), None), P(("grp", "mem")), P(("grp", "mem")))
    return jax.shard_map(
        functools.partial(shards, mesh.size),
        mesh=mesh, in_specs=placed, out_specs=P(("grp", "mem")), check_vma=False,
    )
```

```python
import functools

import jax
import jax.numpy as jnp
from jax import lax
from jax.experimental import pallas as pl
from jax.experimental.pallas import tpu as pltpu
from jax.sharding import PartitionSpec as P

MESH = pl.DeviceIdType.MESH
EPS = 1e-06
LOW = -3.0e38
XS = 4
WAIT_B, STAGE_A = 2, 3
CH = 256

A, B, LO, UP = 0, 1, 2, 3


def kernel(
    blocks, emb, ids, count, out,
    rows, relay, cmeta, rmeta, racc, cacc, vec, got,
    own_sem, sib_sem, up_send, up_recv, lo_send, lo_recv, via_send, via_recv, fwd_send,
    meta_send, meta_recv, vec_send, vec_recv,
):
    n, d = emb.shape
    chunks = n // CH
    half = chunks // 2
    mem = lax.axis_size("mem")
    zs = mem // (2 * 2)
    b = lax.axis_index("grp") * mem + lax.axis_index("mem")

    def device(i):
        i = lax.rem(i + blocks, blocks)
        return (i // mem, lax.rem(i, mem))

    def place(i):
        c = lax.rem(i + blocks, blocks) // 2
        return lax.rem(c // zs, XS), lax.rem(c, zs)

    core = lax.rem(b, 2)
    first, second = core == 0, core == 1
    step = 2 * zs

    def goes_down(i):
        x, z = place(i)
        return (lax.rem(x, 2) == 0) != (z == 0)

    def next_x(i):
        return jnp.where(place(i)[0] == XS - 1, i - (XS - 1) * step, i + step)

    def last_x(i):
        return jnp.where(place(i)[0] == 0, i + (XS - 1) * step, i - step)

    def relay_down(i):
        return jnp.where(place(i)[1] == 0, last_x(i), next_x(i))

    def relay_up(i):
        return jnp.where(place(i)[1] == zs - 1, next_x(i), last_x(i))

    up_down, lo_down = goes_down(b), goes_down(b - 2)
    has_up = jnp.logical_or(first, up_down)
    has_lo = jnp.logical_or(first, jnp.logical_not(lo_down))
    send_down = jnp.logical_or(first, lo_down)
    send_up = jnp.logical_or(second, jnp.logical_not(up_down))
    sibling = b + 1 - 2 * core
    down, up = b - 2, b + 3 - 2 * core
    above, below = b + 2, b - 1 - 2 * core

    via_down = jnp.logical_and(second, lo_down)
    via_up = jnp.logical_and(first, jnp.logical_not(up_down))
    uses_via = jnp.logical_or(via_down, via_up)
    via = jnp.where(first, relay_up(b), relay_down(b))
    z = place(b)[1]
    relay_from = jnp.where(
        jnp.where(first, z == zs - 1, z != 0), last_x(b), next_x(b)
    )
    is_relay = jnp.where(first, jnp.logical_not(goes_down(relay_from)), goes_down(relay_from - 2))
    relay_to = jnp.where(first, relay_from + 3, relay_from - 2)
    split_up = jnp.logical_and(second, has_up)
    split_lo = jnp.logical_and(second, has_lo)
    up_relay, lo_relay = relay_down(b + 2), relay_up(b - 3)

    mine = pl.ds(pl.multiple_of(core * n, n), n)
    own = pltpu.make_async_copy(emb, rows.at[mine], own_sem)
    own.start()

    barrier = pltpu.get_barrier_semaphore()

    def greet(i):
        pl.semaphore_signal(barrier, inc=1, device_id=device(i), device_id_type=MESH)

    for i in (sibling, down, up, above, below):
        greet(i)
    pl.when(is_relay)(lambda: greet(relay_from))
    pl.when(split_up)(lambda: greet(up_relay))
    pl.when(split_lo)(lambda: greet(lo_relay))
    pl.semaphore_wait(barrier, 5 + uses_via.astype(jnp.int32) + is_relay.astype(jnp.int32))

    def copy(src, dst, send, recv, to):
        return pltpu.make_async_remote_copy(
            src_ref=src, dst_ref=dst, send_sem=send, recv_sem=recv, device_id=device(to), device_id_type=MESH
        )

    def part(slot, k):
        return pl.ds(pl.multiple_of(slot * n + k * CH, CH), CH)

    def emb_part(k):
        return emb.at[pl.ds(pl.multiple_of(k * CH, CH), CH)]

    swap = copy(emb, rows.at[mine], sib_sem.at[0], sib_sem.at[1], sibling)
    swap.start()
    downs = [copy(emb_part(k), rows.at[part(UP, k)], up_send.at[k], up_recv.at[k], down) for k in range(chunks)]
    ups = [copy(emb_part(k), rows.at[part(LO, k)], lo_send.at[k], lo_recv.at[k], up) for k in range(chunks)]
    vias = [
        copy(emb_part(half + k), relay.at[pl.ds(k * CH, CH)], via_send.at[k], via_recv.at[k], via) for k in range(half)
    ]
    fwd_up = [
        copy(relay.at[pl.ds(k * CH, CH)], rows.at[part(LO, half + k)], fwd_send.at[k], lo_recv.at[half + k], relay_to)
        for k in range(half)
    ]
    fwd_down = [
        copy(relay.at[pl.ds(k * CH, CH)], rows.at[part(UP, half + k)], fwd_send.at[k], up_recv.at[half + k], relay_to)
        for k in range(half)
    ]
    def send(k):
        if k < half:
            pl.when(uses_via)(vias[k].start)
        pl.when(first)(downs[k].start)
        pl.when(second)(ups[k].start)

    def send_third():
        for k in range(half):
            pl.when(via_down)(downs[k].start)
            pl.when(via_up)(ups[k].start)

    send(0)

    def forward(k):
        pl.when(is_relay)(vias[k].wait_recv)
        pl.when(jnp.logical_and(is_relay, first))(fwd_up[k].start)
        pl.when(jnp.logical_and(is_relay, second))(fwd_down[k].start)

    own.wait()
    cacc[...] = jnp.full(cacc.shape, LOW, jnp.float32)
    racc[...] = jnp.full(racc.shape, LOW, jnp.float32)
    lanes = lax.broadcasted_iota(jnp.int32, (1, n), 1)
    own_ids = ids[...].astype(jnp.float32)
    valid_ids = jnp.where(lanes < count[0], own_ids, -1.0)
    cmeta[1:2, mine] = own_ids
    cmeta[2:3, mine] = valid_ids

    def squares(t, _):
        at = pl.ds(pl.multiple_of(core * n + t * 128, 128), 128)
        block = rows[at, :].astype(jnp.float32)
        scale = lax.rsqrt(jnp.sum(block * block, axis=1, keepdims=True) + EPS)
        wide = jnp.broadcast_to(scale, (128, 128))
        cmeta[0:1, at] = wide.T[0:1]
        return 0

    lax.fori_loop(0, n // 128, squares, 0)

    def spread(slot):
        def group(t, _):
            at = pl.ds(pl.multiple_of(slot * n + t * 128, 128), 128)
            for j in range(3):
                rmeta[j, at, :] = jnp.broadcast_to(cmeta[j : j + 1, at], (128, 128)).T
            return 0

        lax.fori_loop(0, n // 128, group, 0)

    def meta(slot):
        return cmeta.at[:, pl.ds(slot * n, n)]

    meta_sib = copy(cmeta.at[:, mine], cmeta.at[:, mine], meta_send.at[0], meta_recv.at[0], sibling)
    meta_down = copy(cmeta.at[:, mine], meta(UP), meta_send.at[1], meta_recv.at[1], down)
    meta_up = copy(cmeta.at[:, mine], meta(LO), meta_send.at[2], meta_recv.at[2], up)
    meta_sib.start()
    pl.when(send_down)(meta_down.start)
    pl.when(send_up)(meta_up.start)
    for k in range(1, chunks):
        send(k)
    spread(core)

    def dots(row, col):
        return lax.dot_general(
            rows[pl.ds(row, n), :], rows[pl.ds(col, CH), :], (((1,), (1,)), ((), ())),
            preferred_element_type=jnp.float32,
        )

    def fold(values):
        return jnp.max(values.reshape(n // 8, 8, 128), axis=0)

    def lanes_of(col, h):
        return pl.ds(pl.multiple_of(col + h * 128, 128), 128)

    def pair(col, row):
        col, row = pl.multiple_of(col, CH), pl.multiple_of(row, n)
        dot = dots(row, col)
        at = pl.ds(row, n)
        scale, own_id, own_valid = rmeta[0, at, :], rmeta[1, at, :], rmeta[2, at, :]
        row_best = racc[at, :]
        for h in range(CH // 128):
            lane = lanes_of(col, h)
            d = dot[:, h * 128 : (h + 1) * 128]
            row_best = jnp.maximum(row_best, jnp.where(own_id == cmeta[2:3, lane], d * cmeta[0:1, lane], LOW))
            col_best = fold(jnp.where(own_valid == cmeta[1:2, lane], d * scale, LOW))
            cacc[:, lane] = jnp.maximum(cacc[:, lane], col_best)
        racc[at, :] = row_best

    def own_chunk(k, _):
        row = pl.multiple_of(core * n, n)
        col = pl.multiple_of(row + k * CH, CH)
        dot = dots(row, col)
        at = pl.ds(row, n)
        scale, own_valid = rmeta[0, at, :], rmeta[2, at, :]
        apart = lax.broadcasted_iota(jnp.int32, (n, 128), 0) - lax.broadcasted_iota(jnp.int32, (n, 128), 1)
        for h in range(CH // 128):
            lane = lanes_of(col, h)
            d = dot[:, h * 128 : (h + 1) * 128]
            keep = jnp.logical_and(own_valid == cmeta[1:2, lane], apart != k * CH + h * 128)
            cacc[:, lane] = fold(jnp.where(keep, d * scale, LOW))
        return 0

    lax.fori_loop(0, chunks, own_chunk, 0)

    meta_sib.wait_recv()
    theirs = pl.ds(pl.multiple_of(n - core * n, n), n)
    copy(emb, rows.at[theirs], sib_sem.at[0], sib_sem.at[1], sibling).wait_recv()
    spread(1 - core)

    end = chunks + 1

    def stage(e, _):
        arrival = jnp.logical_and(e >= 1, e < end)
        k = jnp.where(first, e - 1, lax.rem(e - 1 + chunks, 2) * half + (e - 1 + chunks) // 2 - half)
        k = jnp.clip(k, 0, chunks - 1)

        @pl.when(e == 1)
        def _():
            pl.when(has_up)(meta_down.wait_recv)
            pl.when(has_up)(lambda: spread(UP))
            pl.when(has_lo)(meta_up.wait_recv)
            pl.when(has_lo)(lambda: spread(LO))

            @pl.when(second)
            def _():
                ups[WAIT_B].wait_send()
                send_third()
                for j in range(half):
                    forward(j)

        @pl.when(jnp.logical_and(first, e == STAGE_A))
        def _():
            send_third()
            for j in range(half):
                forward(j)

        @pl.when(jnp.logical_and(arrival, has_up))
        def _():
            copy(emb_part(k), rows.at[part(UP, k)], up_send.at[k], up_recv.at[k], down).wait_recv()

        @pl.when(jnp.logical_and(arrival, has_lo))
        def _():
            copy(emb_part(k), rows.at[part(LO, k)], lo_send.at[k], lo_recv.at[k], up).wait_recv()

        def unit(j, _):
            slot = jnp.where(j < 2, UP, LO)
            col = jnp.where(arrival, slot * n + k * CH, jnp.where(e == 0, B, LO) * n + j * CH)
            row = jnp.where(arrival, jnp.where(j == 0, A, B), jnp.where(e == 0, A, UP))
            wanted = jnp.where(
                arrival,
                jnp.where(j < 2, has_up, jnp.logical_and(j == 2, jnp.logical_not(lo_down))).astype(jnp.int32),
                jnp.where(e == 0, second, first).astype(jnp.int32),
            )
            pl.when(wanted == 1)(lambda: pair(col, row * n))
            return 0

        lax.fori_loop(0, chunks, unit, 0)
        return 0

    lax.fori_loop(0, end + 1, stage, 0)

    def finish(slot):
        for t in range(n // 128):
            at = pl.ds(pl.multiple_of(slot * n + t * 128, 128), 128)
            best = jnp.maximum(
                jnp.max(racc[at, :].T, axis=0, keepdims=True), jnp.max(cacc[:, at], axis=0, keepdims=True)
            )
            vec[slot, t : t + 1, :] = best * cmeta[0:1, at]

    send_vec_up = copy(vec.at[UP], got.at[1], vec_send.at[1], vec_recv.at[1], above)
    send_vec_lo = copy(vec.at[LO], got.at[2], vec_send.at[2], vec_recv.at[2], below)
    send_vec_sib = copy(vec.at[1 - core], got.at[0], vec_send.at[0], vec_recv.at[0], sibling)

    @pl.when(has_up)
    def _():
        finish(UP)
        send_vec_up.start()

    @pl.when(has_lo)
    def _():
        finish(LO)
        send_vec_lo.start()

    finish(1 - core)
    send_vec_sib.start()
    finish(core)
    best = jnp.maximum(vec[core], -2.0)
    got_down, got_up = send_down, send_up
    send_vec_sib.wait_recv()
    best = jnp.maximum(best, got[0])
    out[...] = best

    @pl.when(got_down)
    def _():
        send_vec_up.wait_recv()
        out[...] = jnp.maximum(out[...], got[1])

    @pl.when(got_up)
    def _():
        send_vec_lo.wait_recv()
        out[...] = jnp.maximum(out[...], got[2])

    swap.wait_send()
    meta_sib.wait_send()
    send_vec_sib.wait_send()
    pl.when(send_down)(meta_down.wait_send)
    pl.when(send_up)(meta_up.wait_send)
    pl.when(has_up)(send_vec_up.wait_send)
    pl.when(has_lo)(send_vec_lo.wait_send)
    for k in range(half):
        pl.when(uses_via)(vias[k].wait_send)
        pl.when(is_relay)(fwd_up[k].wait_send)
    for k in range(chunks):
        pl.when(send_down if k < half else first)(downs[k].wait_send)
        if k == WAIT_B:
            if k < half:
                pl.when(via_up)(ups[k].wait_send)
        else:
            pl.when(send_up if k < half else second)(ups[k].wait_send)


def shards(blocks, embeddings, cluster_ids, valid_counts):
    n, d = embeddings.shape
    chunks = n // CH
    dma = pltpu.SemaphoreType.DMA
    best = pl.pallas_call(
        functools.partial(kernel, blocks),
        out_shape=jax.ShapeDtypeStruct((n // 128, 128), jnp.float32),
        in_specs=[
            pl.BlockSpec(memory_space=pl.ANY),
            pl.BlockSpec(memory_space=pltpu.VMEM),
            pl.BlockSpec(memory_space=pltpu.SMEM),
        ],
        out_specs=pl.BlockSpec(memory_space=pltpu.VMEM),
        scratch_shapes=[
            pltpu.VMEM((4 * n, d), jnp.bfloat16),
            pltpu.VMEM((n // 2, d), jnp.bfloat16),
            pltpu.VMEM((8, 4 * n), jnp.float32),
            pltpu.VMEM((3, 4 * n, 128), jnp.float32),
            pltpu.VMEM((4 * n, 128), jnp.float32),
            pltpu.VMEM((8, 4 * n), jnp.float32),
            pltpu.VMEM((4, n // 128, 128), jnp.float32),
            pltpu.VMEM((3, n // 128, 128), jnp.float32),
            dma(()), dma((2,)),
            dma((chunks,)), dma((chunks,)), dma((chunks,)), dma((chunks,)),
            dma((chunks // 2,)), dma((chunks // 2,)), dma((chunks // 2,)),
            dma((3,)), dma((3,)), dma((3,)), dma((3,)),
        ],
        compiler_params=pltpu.CompilerParams(
            collective_id=0, has_side_effects=True, vmem_limit_bytes=56 * 2**20
        ),
        name="neighbour_cosines",
    )(embeddings, cluster_ids.reshape(1, n), valid_counts)
    return best.reshape(n)


def solution(mesh):
    placed = (P(("grp", "mem"), None), P(("grp", "mem")), P(("grp", "mem")))
    return jax.shard_map(
        functools.partial(shards, mesh.size),
        mesh=mesh, in_specs=placed, out_specs=P(("grp", "mem")), check_vma=False,
    )
```

```python
import functools

import jax
import jax.numpy as jnp
from jax import lax
from jax.experimental import pallas as pl
from jax.experimental.pallas import tpu as pltpu
from jax.sharding import PartitionSpec as P

MESH = pl.DeviceIdType.MESH
EPS = 1e-06
LOW = -3.0e38
XS = 4
WAIT_B, STAGE_A = 2, 3
CH = 256

A, B, LO, UP = 0, 1, 2, 3


def kernel(
    blocks, emb, ids, count, out,
    rows, relay, cmeta, rmeta, racc, cacc, vec, got,
    own_sem, sib_sem, up_send, up_recv, lo_send, lo_recv, via_send, via_recv, fwd_send,
    meta_send, meta_recv, vec_send, vec_recv,
):
    n, d = emb.shape
    chunks = n // CH
    half = chunks // 2
    mem = lax.axis_size("mem")
    zs = mem // (2 * 2)
    b = lax.axis_index("grp") * mem + lax.axis_index("mem")

    def device(i):
        i = lax.rem(i + blocks, blocks)
        return (i // mem, lax.rem(i, mem))

    def place(i):
        c = lax.rem(i + blocks, blocks) // 2
        return lax.rem(c // zs, XS), lax.rem(c, zs)

    core = lax.rem(b, 2)
    first, second = core == 0, core == 1
    step = 2 * zs

    def goes_down(i):
        x, z = place(i)
        return (lax.rem(x, 2) == 0) != (z == 0)

    def next_x(i):
        return jnp.where(place(i)[0] == XS - 1, i - (XS - 1) * step, i + step)

    def last_x(i):
        return jnp.where(place(i)[0] == 0, i + (XS - 1) * step, i - step)

    def relay_down(i):
        return jnp.where(place(i)[1] == 0, last_x(i), next_x(i))

    def relay_up(i):
        return jnp.where(place(i)[1] == zs - 1, next_x(i), last_x(i))

    up_down, lo_down = goes_down(b), goes_down(b - 2)
    has_up = jnp.logical_or(first, up_down)
    has_lo = jnp.logical_or(first, jnp.logical_not(lo_down))
    send_down = jnp.logical_or(first, lo_down)
    send_up = jnp.logical_or(second, jnp.logical_not(up_down))
    sibling = b + 1 - 2 * core
    down, up = b - 2, b + 3 - 2 * core
    above, below = b + 2, b - 1 - 2 * core

    via_down = jnp.logical_and(second, lo_down)
    via_up = jnp.logical_and(first, jnp.logical_not(up_down))
    uses_via = jnp.logical_or(via_down, via_up)
    via = jnp.where(first, relay_up(b), relay_down(b))
    z = place(b)[1]
    relay_from = jnp.where(
        jnp.where(first, z == zs - 1, z != 0), last_x(b), next_x(b)
    )
    is_relay = jnp.where(first, jnp.logical_not(goes_down(relay_from)), goes_down(relay_from - 2))
    relay_to = jnp.where(first, relay_from + 3, relay_from - 2)
    split_up = jnp.logical_and(second, has_up)
    split_lo = jnp.logical_and(second, has_lo)
    up_relay, lo_relay = relay_down(b + 2), relay_up(b - 3)

    mine = pl.ds(pl.multiple_of(core * n, n), n)
    own = pltpu.make_async_copy(emb, rows.at[mine], own_sem)
    own.start()

    barrier = pltpu.get_barrier_semaphore()

    def greet(i):
        pl.semaphore_signal(barrier, inc=1, device_id=device(i), device_id_type=MESH)

    low, high = z == 0, z == zs - 1
    for i in (sibling, down, up, above, below):
        greet(i)
    pl.when(is_relay)(lambda: greet(relay_from))
    pl.when(split_up)(lambda: greet(up_relay))
    pl.when(split_lo)(lambda: greet(lo_relay))
    pl.semaphore_wait(barrier, 5 + uses_via.astype(jnp.int32) + is_relay.astype(jnp.int32))

    def copy(src, dst, send, recv, to):
        return pltpu.make_async_remote_copy(
            src_ref=src, dst_ref=dst, send_sem=send, recv_sem=recv, device_id=device(to), device_id_type=MESH
        )

    def part(slot, k):
        return pl.ds(pl.multiple_of(slot * n + k * CH, CH), CH)

    def emb_part(k):
        return emb.at[pl.ds(pl.multiple_of(k * CH, CH), CH)]

    swap = copy(emb, rows.at[mine], sib_sem.at[0], sib_sem.at[1], sibling)
    swap.start()
    downs = [copy(emb_part(k), rows.at[part(UP, k)], up_send.at[k], up_recv.at[k], down) for k in range(chunks)]
    ups = [copy(emb_part(k), rows.at[part(LO, k)], lo_send.at[k], lo_recv.at[k], up) for k in range(chunks)]
    vias = [
        copy(emb_part(half + k), relay.at[pl.ds(k * CH, CH)], via_send.at[k], via_recv.at[k], via) for k in range(half)
    ]
    fwd_up = [
        copy(relay.at[pl.ds(k * CH, CH)], rows.at[part(LO, half + k)], fwd_send.at[k], lo_recv.at[half + k], relay_to)
        for k in range(half)
    ]
    fwd_down = [
        copy(relay.at[pl.ds(k * CH, CH)], rows.at[part(UP, half + k)], fwd_send.at[k], up_recv.at[half + k], relay_to)
        for k in range(half)
    ]
    def send(k):
        if k < half:
            pl.when(uses_via)(vias[k].start)
        pl.when(first)(downs[k].start)
        pl.when(second)(ups[k].start)

    def send_third():
        for k in range(half):
            pl.when(via_down)(downs[k].start)
            pl.when(via_up)(ups[k].start)

    send(0)

    def forward(k):
        pl.when(is_relay)(vias[k].wait_recv)
        pl.when(jnp.logical_and(is_relay, first))(fwd_up[k].start)
        pl.when(jnp.logical_and(is_relay, second))(fwd_down[k].start)

    own.wait()
    cacc[...] = jnp.full(cacc.shape, LOW, jnp.float32)
    racc[...] = jnp.full(racc.shape, LOW, jnp.float32)
    lanes = lax.broadcasted_iota(jnp.int32, (1, n), 1)
    own_ids = ids[...].astype(jnp.float32)
    valid_ids = jnp.where(lanes < count[0], own_ids, -1.0)
    cmeta[1:2, mine] = own_ids
    cmeta[2:3, mine] = valid_ids

    def squares(t, _):
        at = pl.ds(pl.multiple_of(core * n + t * 128, 128), 128)
        block = rows[at, :].astype(jnp.float32)
        scale = lax.rsqrt(jnp.sum(block * block, axis=1, keepdims=True) + EPS)
        wide = jnp.broadcast_to(scale, (128, 128))
        cmeta[0:1, at] = wide.T[0:1]
        return 0

    lax.fori_loop(0, n // 128, squares, 0)

    def spread(slot):
        def group(t, _):
            at = pl.ds(pl.multiple_of(slot * n + t * 128, 128), 128)
            for j in range(3):
                rmeta[j, at, :] = jnp.broadcast_to(cmeta[j : j + 1, at], (128, 128)).T
            return 0

        lax.fori_loop(0, n // 128, group, 0)

    def meta(slot):
        return cmeta.at[:, pl.ds(slot * n, n)]

    meta_sib = copy(cmeta.at[:, mine], cmeta.at[:, mine], meta_send.at[0], meta_recv.at[0], sibling)
    meta_down = copy(cmeta.at[:, mine], meta(UP), meta_send.at[1], meta_recv.at[1], down)
    meta_up = copy(cmeta.at[:, mine], meta(LO), meta_send.at[2], meta_recv.at[2], up)
    meta_sib.start()
    pl.when(send_down)(meta_down.start)
    pl.when(send_up)(meta_up.start)
    for k in range(1, chunks):
        send(k)
    spread(core)

    def dots(row, col):
        return lax.dot_general(
            rows[pl.ds(row, n), :], rows[pl.ds(col, CH), :], (((1,), (1,)), ((), ())),
            preferred_element_type=jnp.float32,
        )

    def fold(values):
        return jnp.max(values.reshape(n // 8, 8, 128), axis=0)

    def lanes_of(col, h):
        return pl.ds(pl.multiple_of(col + h * 128, 128), 128)

    def pair(col, row):
        col, row = pl.multiple_of(col, CH), pl.multiple_of(row, n)
        dot = dots(row, col)
        at = pl.ds(row, n)
        scale, own_id, own_valid = rmeta[0, at, :], rmeta[1, at, :], rmeta[2, at, :]
        row_best = racc[at, :]
        for h in range(CH // 128):
            lane = lanes_of(col, h)
            d = dot[:, h * 128 : (h + 1) * 128]
            row_best = jnp.maximum(row_best, jnp.where(own_id == cmeta[2:3, lane], d * cmeta[0:1, lane], LOW))
            col_best = fold(jnp.where(own_valid == cmeta[1:2, lane], d * scale, LOW))
            cacc[:, lane] = jnp.maximum(cacc[:, lane], col_best)
        racc[at, :] = row_best

    def own_chunk(k, _):
        row = pl.multiple_of(core * n, n)
        col = pl.multiple_of(row + k * CH, CH)
        dot = dots(row, col)
        at = pl.ds(row, n)
        scale, own_valid = rmeta[0, at, :], rmeta[2, at, :]
        apart = lax.broadcasted_iota(jnp.int32, (n, 128), 0) - lax.broadcasted_iota(jnp.int32, (n, 128), 1)
        for h in range(CH // 128):
            lane = lanes_of(col, h)
            d = dot[:, h * 128 : (h + 1) * 128]
            keep = jnp.logical_and(own_valid == cmeta[1:2, lane], apart != k * CH + h * 128)
            cacc[:, lane] = fold(jnp.where(keep, d * scale, LOW))
        return 0

    lax.fori_loop(0, chunks, own_chunk, 0)

    meta_sib.wait_recv()
    theirs = pl.ds(pl.multiple_of(n - core * n, n), n)
    copy(emb, rows.at[theirs], sib_sem.at[0], sib_sem.at[1], sibling).wait_recv()
    spread(1 - core)

    def finish(slot):
        for t in range(n // 128):
            at = pl.ds(pl.multiple_of(slot * n + t * 128, 128), 128)
            best = jnp.maximum(
                jnp.max(racc[at, :].T, axis=0, keepdims=True), jnp.max(cacc[:, at], axis=0, keepdims=True)
            )
            vec[slot, t : t + 1, :] = best * cmeta[0:1, at]

    send_vec_up = copy(vec.at[UP], got.at[1], vec_send.at[1], vec_recv.at[1], above)
    send_vec_lo = copy(vec.at[LO], got.at[2], vec_send.at[2], vec_recv.at[2], below)
    send_vec_sib = copy(vec.at[1 - core], got.at[0], vec_send.at[0], vec_recv.at[0], sibling)

    def stage(e, _):
        arrival = e >= 1
        k = jnp.maximum(e - 1, 0)
        k = jnp.where(first, k, lax.rem(k, 2) * half + k // 2)

        @pl.when(e == 1)
        def _():
            pl.when(has_up)(meta_down.wait_recv)
            pl.when(has_up)(lambda: spread(UP))
            pl.when(has_lo)(meta_up.wait_recv)
            pl.when(has_lo)(lambda: spread(LO))

            @pl.when(second)
            def _():
                ups[WAIT_B].wait_send()
                send_third()
                for j in range(half):
                    forward(j)

        @pl.when(jnp.logical_and(first, e == jnp.where(high, 2, STAGE_A)))
        def _():
            send_third()
            for j in range(half):
                forward(j)

        full = e == chunks

        def unit(j, _):
            newest = j >= chunks

            @pl.when(jnp.logical_and(jnp.logical_and(arrival, j == 0), has_lo))
            def _():
                copy(emb_part(k), rows.at[part(LO, k)], lo_send.at[k], lo_recv.at[k], up).wait_recv()

            @pl.when(jnp.logical_and(jnp.logical_and(arrival, j == chunks), has_up))
            def _():
                copy(emb_part(k), rows.at[part(UP, k)], up_send.at[k], up_recv.at[k], down).wait_recv()

            from_lo = jnp.logical_and(arrival, j == 0)
            slot = jnp.where(arrival, jnp.where(from_lo, LO, UP), B)
            chunk = jnp.where(arrival, jnp.where(jnp.logical_or(from_lo, newest), k, j - 1), j)
            row = jnp.where(
                arrival, jnp.where(from_lo, B, jnp.where(newest, jnp.where(j == chunks + 2, LO, j - chunks), LO)), A
            )
            crossing = jnp.logical_and(first, full)
            wanted = jnp.where(
                arrival,
                jnp.where(
                    from_lo,
                    jnp.logical_not(lo_down).astype(jnp.int32),
                    jnp.where(
                        jnp.logical_and(newest, j < chunks + 2), has_up.astype(jnp.int32), crossing.astype(jnp.int32)
                    ),
                ),
                jnp.logical_and(second, j < chunks).astype(jnp.int32),
            )
            pl.when(wanted == 1)(lambda: pair(slot * n + chunk * CH, row * n))

            @pl.when(jnp.logical_and(jnp.logical_and(has_lo, full), j == (chunks + 2) * (1 - core)))
            def _():
                finish(LO)
                send_vec_lo.start()

            return 0

        lax.fori_loop(0, chunks + 3, unit, 0)
        return 0

    lax.fori_loop(0, chunks + 1, stage, 0)

    @pl.when(has_up)
    def _():
        finish(UP)
        send_vec_up.start()

    finish(1 - core)
    send_vec_sib.start()
    finish(core)
    best = vec[core]
    got_down, got_up = send_down, send_up
    send_vec_sib.wait_recv()
    best = jnp.maximum(best, got[0])
    out[...] = best

    @pl.when(got_down)
    def _():
        send_vec_up.wait_recv()
        out[...] = jnp.maximum(out[...], got[1])

    @pl.when(got_up)
    def _():
        send_vec_lo.wait_recv()
        out[...] = jnp.maximum(out[...], got[2])

    swap.wait_send()
    meta_sib.wait_send()
    send_vec_sib.wait_send()
    pl.when(send_down)(meta_down.wait_send)
    pl.when(send_up)(meta_up.wait_send)
    pl.when(has_up)(send_vec_up.wait_send)
    pl.when(has_lo)(send_vec_lo.wait_send)
    for k in range(half):
        pl.when(uses_via)(vias[k].wait_send)
        pl.when(is_relay)(fwd_up[k].wait_send)
    for k in range(chunks):
        pl.when(send_down if k < half else first)(downs[k].wait_send)
        if k == WAIT_B:
            if k < half:
                pl.when(via_up)(ups[k].wait_send)
        else:
            pl.when(send_up if k < half else second)(ups[k].wait_send)


def shards(blocks, embeddings, cluster_ids, valid_counts):
    n, d = embeddings.shape
    chunks = n // CH
    dma = pltpu.SemaphoreType.DMA
    best = pl.pallas_call(
        functools.partial(kernel, blocks),
        out_shape=jax.ShapeDtypeStruct((n // 128, 128), jnp.float32),
        in_specs=[
            pl.BlockSpec(memory_space=pl.ANY),
            pl.BlockSpec(memory_space=pltpu.VMEM),
            pl.BlockSpec(memory_space=pltpu.SMEM),
        ],
        out_specs=pl.BlockSpec(memory_space=pltpu.VMEM),
        scratch_shapes=[
            pltpu.VMEM((4 * n, d), jnp.bfloat16),
            pltpu.VMEM((n // 2, d), jnp.bfloat16),
            pltpu.VMEM((8, 4 * n), jnp.float32),
            pltpu.VMEM((3, 4 * n, 128), jnp.float32),
            pltpu.VMEM((4 * n, 128), jnp.float32),
            pltpu.VMEM((8, 4 * n), jnp.float32),
            pltpu.VMEM((4, n // 128, 128), jnp.float32),
            pltpu.VMEM((3, n // 128, 128), jnp.float32),
            dma(()), dma((2,)),
            dma((chunks,)), dma((chunks,)), dma((chunks,)), dma((chunks,)),
            dma((chunks // 2,)), dma((chunks // 2,)), dma((chunks // 2,)),
            dma((3,)), dma((3,)), dma((3,)), dma((3,)),
        ],
        compiler_params=pltpu.CompilerParams(
            collective_id=0, has_side_effects=True, vmem_limit_bytes=56 * 2**20
        ),
        name="neighbour_cosines",
    )(embeddings, cluster_ids.reshape(1, n), valid_counts)
    return lax.optimization_barrier(jnp.maximum(best, -2.0)).reshape(n)


def solution(mesh):
    placed = (P(("grp", "mem"), None), P(("grp", "mem")), P(("grp", "mem")))
    return jax.shard_map(
        functools.partial(shards, mesh.size),
        mesh=mesh, in_specs=placed, out_specs=P(("grp", "mem")), check_vma=False,
    )
```

```python
import functools

import jax
import jax.numpy as jnp
from jax import lax
from jax.experimental import pallas as pl
from jax.experimental.pallas import tpu as pltpu
from jax.sharding import PartitionSpec as P

MESH = pl.DeviceIdType.MESH
EPS = 1e-06
LOW = -3.0e38
XS = 4
WAIT_B, STAGE_A = 2, 3
CH = 256

A, B, LO, UP = 0, 1, 2, 3


def kernel(
    blocks, emb, ids, count, out,
    rows, relay, cmeta, rmeta, racc, cacc, vec, got,
    own_sem, sib_sem, up_send, up_recv, lo_send, lo_recv, via_send, via_recv, fwd_send,
    meta_send, meta_recv, vec_send, vec_recv,
):
    n, d = emb.shape
    chunks = n // CH
    half = chunks // 2
    mem = lax.axis_size("mem")
    zs = mem // (2 * 2)
    b = lax.axis_index("grp") * mem + lax.axis_index("mem")

    def device(i):
        i = lax.rem(i + blocks, blocks)
        return (i // mem, lax.rem(i, mem))

    def place(i):
        c = lax.rem(i + blocks, blocks) // 2
        return lax.rem(c // zs, XS), lax.rem(c, zs)

    core = lax.rem(b, 2)
    first, second = core == 0, core == 1
    step = 2 * zs

    def goes_down(i):
        x, z = place(i)
        return (lax.rem(x, 2) == 0) != (z == 0)

    def next_x(i):
        return jnp.where(place(i)[0] == XS - 1, i - (XS - 1) * step, i + step)

    def last_x(i):
        return jnp.where(place(i)[0] == 0, i + (XS - 1) * step, i - step)

    def relay_down(i):
        return jnp.where(place(i)[1] == 0, last_x(i), next_x(i))

    def relay_up(i):
        return jnp.where(place(i)[1] == zs - 1, next_x(i), last_x(i))

    up_down, lo_down = goes_down(b), goes_down(b - 2)
    has_up = jnp.logical_or(first, up_down)
    has_lo = jnp.logical_or(first, jnp.logical_not(lo_down))
    send_down = jnp.logical_or(first, lo_down)
    send_up = jnp.logical_or(second, jnp.logical_not(up_down))
    sibling = b + 1 - 2 * core
    down, up = b - 2, b + 3 - 2 * core
    above, below = b + 2, b - 1 - 2 * core

    via_down = jnp.logical_and(second, lo_down)
    via_up = jnp.logical_and(first, jnp.logical_not(up_down))
    uses_via = jnp.logical_or(via_down, via_up)
    via = jnp.where(first, relay_up(b), relay_down(b))
    z = place(b)[1]
    relay_from = jnp.where(
        jnp.where(first, z == zs - 1, z != 0), last_x(b), next_x(b)
    )
    is_relay = jnp.where(first, jnp.logical_not(goes_down(relay_from)), goes_down(relay_from - 2))
    relay_to = jnp.where(first, relay_from + 3, relay_from - 2)
    split_up = jnp.logical_and(second, has_up)
    split_lo = jnp.logical_and(second, has_lo)
    up_relay, lo_relay = relay_down(b + 2), relay_up(b - 3)

    mine = pl.ds(pl.multiple_of(core * n, n), n)
    own = pltpu.make_async_copy(emb, rows.at[mine], own_sem)
    own.start()

    barrier = pltpu.get_barrier_semaphore()

    def greet(i):
        pl.semaphore_signal(barrier, inc=1, device_id=device(i), device_id_type=MESH)

    low, high = z == 0, z == zs - 1
    for i in (sibling, down, up, above, below):
        greet(i)
    pl.when(is_relay)(lambda: greet(relay_from))
    pl.when(split_up)(lambda: greet(up_relay))
    pl.when(split_lo)(lambda: greet(lo_relay))
    pl.semaphore_wait(barrier, 5 + uses_via.astype(jnp.int32) + is_relay.astype(jnp.int32))

    def copy(src, dst, send, recv, to):
        return pltpu.make_async_remote_copy(
            src_ref=src, dst_ref=dst, send_sem=send, recv_sem=recv, device_id=device(to), device_id_type=MESH
        )

    def part(slot, k):
        return pl.ds(pl.multiple_of(slot * n + k * CH, CH), CH)

    def emb_part(k):
        return emb.at[pl.ds(pl.multiple_of(k * CH, CH), CH)]

    swap = copy(emb, rows.at[mine], sib_sem.at[0], sib_sem.at[1], sibling)
    swap.start()
    downs = [copy(emb_part(k), rows.at[part(UP, k)], up_send.at[k], up_recv.at[k], down) for k in range(chunks)]
    ups = [copy(emb_part(k), rows.at[part(LO, k)], lo_send.at[k], lo_recv.at[k], up) for k in range(chunks)]
    vias = [
        copy(emb_part(half + k), relay.at[pl.ds(k * CH, CH)], via_send.at[k], via_recv.at[k], via) for k in range(half)
    ]
    fwd_up = [
        copy(relay.at[pl.ds(k * CH, CH)], rows.at[part(LO, half + k)], fwd_send.at[k], lo_recv.at[half + k], relay_to)
        for k in range(half)
    ]
    fwd_down = [
        copy(relay.at[pl.ds(k * CH, CH)], rows.at[part(UP, half + k)], fwd_send.at[k], up_recv.at[half + k], relay_to)
        for k in range(half)
    ]
    def send(k):
        if k < half:
            pl.when(uses_via)(vias[k].start)
        pl.when(first)(downs[k].start)
        pl.when(second)(ups[k].start)

    def send_third():
        for k in range(half):
            pl.when(via_down)(downs[k].start)
            pl.when(via_up)(ups[k].start)

    send(0)

    def forward(k):
        pl.when(is_relay)(vias[k].wait_recv)
        pl.when(jnp.logical_and(is_relay, first))(fwd_up[k].start)
        pl.when(jnp.logical_and(is_relay, second))(fwd_down[k].start)

    own.wait()
    cacc[...] = jnp.full(cacc.shape, LOW, jnp.float32)
    racc[...] = jnp.full(racc.shape, LOW, jnp.float32)
    lanes = lax.broadcasted_iota(jnp.int32, (1, n), 1)
    own_ids = ids[...].astype(jnp.float32)
    valid_ids = jnp.where(lanes < count[0], own_ids, -1.0)
    cmeta[1:2, mine] = own_ids
    cmeta[2:3, mine] = valid_ids

    def squares(t, _):
        at = pl.ds(pl.multiple_of(core * n + t * 128, 128), 128)
        block = rows[at, :].astype(jnp.float32)
        scale = lax.rsqrt(jnp.sum(block * block, axis=1, keepdims=True) + EPS)
        wide = jnp.broadcast_to(scale, (128, 128))
        cmeta[0:1, at] = wide.T[0:1]
        return 0

    lax.fori_loop(0, n // 128, squares, 0)

    def spread(slot):
        def group(t, _):
            at = pl.ds(pl.multiple_of(slot * n + t * 128, 128), 128)
            for j in range(3):
                rmeta[j, at, :] = jnp.broadcast_to(cmeta[j : j + 1, at], (128, 128)).T
            return 0

        lax.fori_loop(0, n // 128, group, 0)

    def meta(slot):
        return cmeta.at[:, pl.ds(slot * n, n)]

    meta_sib = copy(cmeta.at[:, mine], cmeta.at[:, mine], meta_send.at[0], meta_recv.at[0], sibling)
    meta_down = copy(cmeta.at[:, mine], meta(UP), meta_send.at[1], meta_recv.at[1], down)
    meta_up = copy(cmeta.at[:, mine], meta(LO), meta_send.at[2], meta_recv.at[2], up)
    meta_sib.start()
    pl.when(send_down)(meta_down.start)
    pl.when(send_up)(meta_up.start)
    for k in range(1, chunks):
        send(k)
    spread(core)

    def dots(row, col):
        return lax.dot_general(
            rows[pl.ds(row, n), :], rows[pl.ds(col, CH), :], (((1,), (1,)), ((), ())),
            preferred_element_type=jnp.float32,
        )

    def fold(values):
        return jnp.max(values.reshape(n // 8, 8, 128), axis=0)

    def lanes_of(col, h):
        return pl.ds(pl.multiple_of(col + h * 128, 128), 128)

    def pair(col, row):
        col, row = pl.multiple_of(col, CH), pl.multiple_of(row, n)
        dot = dots(row, col)
        at = pl.ds(row, n)
        scale, own_id, own_valid = rmeta[0, at, :], rmeta[1, at, :], rmeta[2, at, :]
        row_best = racc[at, :]
        for h in range(CH // 128):
            lane = lanes_of(col, h)
            d = dot[:, h * 128 : (h + 1) * 128]
            row_best = jnp.maximum(row_best, jnp.where(own_id == cmeta[2:3, lane], d * cmeta[0:1, lane], LOW))
            col_best = fold(jnp.where(own_valid == cmeta[1:2, lane], d * scale, LOW))
            cacc[:, lane] = jnp.maximum(cacc[:, lane], col_best)
        racc[at, :] = row_best

    def own_chunk(k, _):
        row = pl.multiple_of(core * n, n)
        col = pl.multiple_of(row + k * CH, CH)
        dot = dots(row, col)
        at = pl.ds(row, n)
        scale, own_valid = rmeta[0, at, :], rmeta[2, at, :]
        apart = lax.broadcasted_iota(jnp.int32, (n, 128), 0) - lax.broadcasted_iota(jnp.int32, (n, 128), 1)
        for h in range(CH // 128):
            lane = lanes_of(col, h)
            d = dot[:, h * 128 : (h + 1) * 128]
            keep = jnp.logical_and(own_valid == cmeta[1:2, lane], apart != k * CH + h * 128)
            cacc[:, lane] = fold(jnp.where(keep, d * scale, LOW))
        return 0

    lax.fori_loop(0, chunks, own_chunk, 0)

    meta_sib.wait_recv()
    theirs = pl.ds(pl.multiple_of(n - core * n, n), n)
    copy(emb, rows.at[theirs], sib_sem.at[0], sib_sem.at[1], sibling).wait_recv()
    spread(1 - core)

    def finish(slot):
        for t in range(n // 128):
            at = pl.ds(pl.multiple_of(slot * n + t * 128, 128), 128)
            best = jnp.max(cacc[:, at], axis=0, keepdims=True)
            if not (isinstance(slot, int) and slot == UP):
                best = jnp.maximum(best, jnp.max(racc[at, :].T, axis=0, keepdims=True))
            vec[slot, t : t + 1, :] = best * cmeta[0:1, at]

    send_vec_up = copy(vec.at[UP], got.at[1], vec_send.at[1], vec_recv.at[1], above)
    send_vec_lo = copy(vec.at[LO], got.at[2], vec_send.at[2], vec_recv.at[2], below)
    send_vec_sib = copy(vec.at[1 - core], got.at[0], vec_send.at[0], vec_recv.at[0], sibling)

    def stage(e, _):
        arrival = e >= 1
        k = jnp.maximum(e - 1, 0)
        k = jnp.where(first, k, lax.rem(k, 2) * half + k // 2)

        @pl.when(e == 1)
        def _():
            pl.when(has_up)(meta_down.wait_recv)
            pl.when(has_up)(lambda: spread(UP))
            pl.when(has_lo)(meta_up.wait_recv)
            pl.when(has_lo)(lambda: spread(LO))

            @pl.when(second)
            def _():
                ups[WAIT_B].wait_send()
                send_third()
                for j in range(half):
                    forward(j)

        @pl.when(jnp.logical_and(first, e == jnp.where(high, 2, STAGE_A)))
        def _():
            send_third()
            for j in range(half):
                forward(j)

        full = e == chunks

        def unit(j, _):
            newest = j >= chunks

            @pl.when(jnp.logical_and(jnp.logical_and(arrival, j == 0), has_lo))
            def _():
                copy(emb_part(k), rows.at[part(LO, k)], lo_send.at[k], lo_recv.at[k], up).wait_recv()

            @pl.when(jnp.logical_and(jnp.logical_and(arrival, j == chunks), has_up))
            def _():
                copy(emb_part(k), rows.at[part(UP, k)], up_send.at[k], up_recv.at[k], down).wait_recv()

            from_lo = jnp.logical_and(arrival, j == 0)
            slot = jnp.where(arrival, jnp.where(from_lo, LO, UP), B)
            chunk = jnp.where(arrival, jnp.where(jnp.logical_or(from_lo, newest), k, j - 1), j)
            row = jnp.where(
                arrival, jnp.where(from_lo, B, jnp.where(j > chunks, j - chunks - 1, LO)), A
            )
            crossing = jnp.logical_and(first, full)
            wanted = jnp.where(
                arrival,
                jnp.where(
                    from_lo,
                    jnp.logical_not(lo_down).astype(jnp.int32),
                    jnp.where(
                        j > chunks, has_up.astype(jnp.int32), crossing.astype(jnp.int32)
                    ),
                ),
                jnp.logical_and(second, j < chunks).astype(jnp.int32),
            )
            pl.when(wanted == 1)(lambda: pair(slot * n + chunk * CH, row * n))

            @pl.when(jnp.logical_and(jnp.logical_and(has_lo, full), j == chunks * (1 - core)))
            def _():
                finish(LO)
                send_vec_lo.start()

            return 0

        lax.fori_loop(0, chunks + 3, unit, 0)
        return 0

    lax.fori_loop(0, chunks + 1, stage, 0)

    @pl.when(has_up)
    def _():
        finish(UP)
        send_vec_up.start()

    finish(1 - core)
    send_vec_sib.start()
    finish(core)
    best = vec[core]
    got_down, got_up = send_down, send_up
    send_vec_sib.wait_recv()
    best = jnp.maximum(best, got[0])
    out[...] = best

    @pl.when(got_down)
    def _():
        send_vec_up.wait_recv()
        out[...] = jnp.maximum(out[...], got[1])

    @pl.when(got_up)
    def _():
        send_vec_lo.wait_recv()
        out[...] = jnp.maximum(out[...], got[2])

    swap.wait_send()
    meta_sib.wait_send()
    send_vec_sib.wait_send()
    pl.when(send_down)(meta_down.wait_send)
    pl.when(send_up)(meta_up.wait_send)
    pl.when(has_up)(send_vec_up.wait_send)
    pl.when(has_lo)(send_vec_lo.wait_send)
    for k in range(half):
        pl.when(uses_via)(vias[k].wait_send)
        pl.when(is_relay)(fwd_up[k].wait_send)
    for k in range(chunks):
        pl.when(send_down if k < half else first)(downs[k].wait_send)
        if k == WAIT_B:
            if k < half:
                pl.when(via_up)(ups[k].wait_send)
        else:
            pl.when(send_up if k < half else second)(ups[k].wait_send)


def shards(blocks, embeddings, cluster_ids, valid_counts):
    n, d = embeddings.shape
    chunks = n // CH
    dma = pltpu.SemaphoreType.DMA
    best = pl.pallas_call(
        functools.partial(kernel, blocks),
        out_shape=jax.ShapeDtypeStruct((n // 128, 128), jnp.float32),
        in_specs=[
            pl.BlockSpec(memory_space=pl.ANY),
            pl.BlockSpec(memory_space=pltpu.VMEM),
            pl.BlockSpec(memory_space=pltpu.SMEM),
        ],
        out_specs=pl.BlockSpec(memory_space=pltpu.VMEM),
        scratch_shapes=[
            pltpu.VMEM((4 * n, d), jnp.bfloat16),
            pltpu.VMEM((n // 2, d), jnp.bfloat16),
            pltpu.VMEM((8, 4 * n), jnp.float32),
            pltpu.VMEM((3, 4 * n, 128), jnp.float32),
            pltpu.VMEM((4 * n, 128), jnp.float32),
            pltpu.VMEM((8, 4 * n), jnp.float32),
            pltpu.VMEM((4, n // 128, 128), jnp.float32),
            pltpu.VMEM((3, n // 128, 128), jnp.float32),
            dma(()), dma((2,)),
            dma((chunks,)), dma((chunks,)), dma((chunks,)), dma((chunks,)),
            dma((chunks // 2,)), dma((chunks // 2,)), dma((chunks // 2,)),
            dma((3,)), dma((3,)), dma((3,)), dma((3,)),
        ],
        compiler_params=pltpu.CompilerParams(
            collective_id=0, has_side_effects=True, vmem_limit_bytes=53 * 2**20
        ),
        name="neighbour_cosines",
    )(embeddings, cluster_ids.reshape(1, n), valid_counts)
    return lax.optimization_barrier(jnp.maximum(best, -2.0)).reshape(n)


def solution(mesh):
    placed = (P(("grp", "mem"), None), P(("grp", "mem")), P(("grp", "mem")))
    return jax.shard_map(
        functools.partial(shards, mesh.size),
        mesh=mesh, in_specs=placed, out_specs=P(("grp", "mem")), check_vma=False,
    )
```

```python
import functools

import jax
import jax.numpy as jnp
from jax import lax
from jax.experimental import pallas as pl
from jax.experimental.pallas import tpu as pltpu
from jax.sharding import PartitionSpec as P

MESH = pl.DeviceIdType.MESH
EPS = 1e-06
LOW = -3.0e38
XS = 4
WAIT_B, STAGE_A = 2, 3
CH = 256

A, B, LO, UP = 0, 1, 2, 3


def kernel(
    blocks, emb, ids, count, out,
    rows, relay, cmeta, rmeta, racc, cacc, vec, got,
    own_sem, sib_sem, up_send, up_recv, lo_send, lo_recv, via_send, via_recv, fwd_send,
    meta_send, meta_recv, vec_send, vec_recv,
):
    n, d = emb.shape
    chunks = n // CH
    half = chunks // 2
    mem = lax.axis_size("mem")
    zs = mem // (2 * 2)
    b = lax.axis_index("grp") * mem + lax.axis_index("mem")

    def device(i):
        i = lax.rem(i + blocks, blocks)
        return (i // mem, lax.rem(i, mem))

    def place(i):
        c = lax.rem(i + blocks, blocks) // 2
        return lax.rem(c // zs, XS), lax.rem(c, zs)

    core = lax.rem(b, 2)
    first, second = core == 0, core == 1
    step = 2 * zs

    def goes_down(i):
        x, z = place(i)
        return (lax.rem(x, 2) == 0) != (z == 0)

    def next_x(i):
        return jnp.where(place(i)[0] == XS - 1, i - (XS - 1) * step, i + step)

    def last_x(i):
        return jnp.where(place(i)[0] == 0, i + (XS - 1) * step, i - step)

    def relay_down(i):
        return jnp.where(place(i)[1] == 0, last_x(i), next_x(i))

    def relay_up(i):
        return jnp.where(place(i)[1] == zs - 1, next_x(i), last_x(i))

    up_down, lo_down = goes_down(b), goes_down(b - 2)
    has_up = jnp.logical_or(first, up_down)
    has_lo = jnp.logical_or(first, jnp.logical_not(lo_down))
    send_down = jnp.logical_or(first, lo_down)
    send_up = jnp.logical_or(second, jnp.logical_not(up_down))
    sibling = b + 1 - 2 * core
    down, up = b - 2, b + 3 - 2 * core
    above, below = b + 2, b - 1 - 2 * core

    via_down = jnp.logical_and(second, lo_down)
    via_up = jnp.logical_and(first, jnp.logical_not(up_down))
    uses_via = jnp.logical_or(via_down, via_up)
    via = jnp.where(first, relay_up(b), relay_down(b))
    z = place(b)[1]
    relay_from = jnp.where(
        jnp.where(first, z == zs - 1, z != 0), last_x(b), next_x(b)
    )
    is_relay = jnp.where(first, jnp.logical_not(goes_down(relay_from)), goes_down(relay_from - 2))
    relay_to = jnp.where(first, relay_from + 3, relay_from - 2)
    split_up = jnp.logical_and(second, has_up)
    split_lo = jnp.logical_and(second, has_lo)
    up_relay, lo_relay = relay_down(b + 2), relay_up(b - 3)

    mine = pl.ds(pl.multiple_of(core * n, n), n)
    own = pltpu.make_async_copy(emb, rows.at[mine], own_sem)
    own.start()

    barrier = pltpu.get_barrier_semaphore()

    def greet(i):
        pl.semaphore_signal(barrier, inc=1, device_id=device(i), device_id_type=MESH)

    low, high = z == 0, z == zs - 1
    for i in (sibling, down, up, above, below):
        greet(i)
    pl.when(is_relay)(lambda: greet(relay_from))
    pl.when(split_up)(lambda: greet(up_relay))
    pl.when(split_lo)(lambda: greet(lo_relay))
    pl.semaphore_wait(barrier, 5 + uses_via.astype(jnp.int32) + is_relay.astype(jnp.int32))

    def copy(src, dst, send, recv, to):
        return pltpu.make_async_remote_copy(
            src_ref=src, dst_ref=dst, send_sem=send, recv_sem=recv, device_id=device(to), device_id_type=MESH
        )

    def part(slot, k):
        return pl.ds(pl.multiple_of(slot * n + k * CH, CH), CH)

    def emb_part(k):
        return emb.at[pl.ds(pl.multiple_of(k * CH, CH), CH)]

    swap = copy(emb, rows.at[mine], sib_sem.at[0], sib_sem.at[1], sibling)
    swap.start()
    downs = [copy(emb_part(k), rows.at[part(UP, k)], up_send.at[k], up_recv.at[k], down) for k in range(chunks)]
    ups = [copy(emb_part(k), rows.at[part(LO, k)], lo_send.at[k], lo_recv.at[k], up) for k in range(chunks)]
    vias = [
        copy(emb_part(half + k), relay.at[pl.ds(k * CH, CH)], via_send.at[k], via_recv.at[k], via) for k in range(half)
    ]
    fwd_up = [
        copy(relay.at[pl.ds(k * CH, CH)], rows.at[part(LO, half + k)], fwd_send.at[k], lo_recv.at[half + k], relay_to)
        for k in range(half)
    ]
    fwd_down = [
        copy(relay.at[pl.ds(k * CH, CH)], rows.at[part(UP, half + k)], fwd_send.at[k], up_recv.at[half + k], relay_to)
        for k in range(half)
    ]
    def send(k):
        if k < half:
            pl.when(uses_via)(vias[k].start)
        pl.when(first)(downs[k].start)
        pl.when(second)(ups[k].start)

    def send_third():
        for k in range(half):
            pl.when(via_down)(downs[k].start)
            pl.when(via_up)(ups[k].start)

    send(0)

    def forward(k):
        pl.when(is_relay)(vias[k].wait_recv)
        pl.when(jnp.logical_and(is_relay, first))(fwd_up[k].start)
        pl.when(jnp.logical_and(is_relay, second))(fwd_down[k].start)

    own.wait()
    cacc[...] = jnp.full(cacc.shape, LOW, jnp.float32)
    racc[...] = jnp.full(racc.shape, LOW, jnp.float32)
    lanes = lax.broadcasted_iota(jnp.int32, (1, n), 1)
    own_ids = ids[...].astype(jnp.float32)
    valid_ids = jnp.where(lanes < count[0], own_ids, -1.0)
    cmeta[1:2, mine] = own_ids
    cmeta[2:3, mine] = valid_ids

    def squares(t, _):
        at = pl.ds(pl.multiple_of(core * n + t * 128, 128), 128)
        block = rows[at, :].astype(jnp.float32)
        scale = lax.rsqrt(jnp.sum(block * block, axis=1, keepdims=True) + EPS)
        wide = jnp.broadcast_to(scale, (128, 128))
        cmeta[0:1, at] = wide.T[0:1]
        return 0

    lax.fori_loop(0, n // 128, squares, 0)

    def spread(slot):
        def group(t, _):
            at = pl.ds(pl.multiple_of(slot * n + t * 128, 128), 128)
            for j in range(3):
                rmeta[j, at, :] = jnp.broadcast_to(cmeta[j : j + 1, at], (128, 128)).T
            return 0

        lax.fori_loop(0, n // 128, group, 0)

    def meta(slot):
        return cmeta.at[:, pl.ds(slot * n, n)]

    meta_sib = copy(cmeta.at[:, mine], cmeta.at[:, mine], meta_send.at[0], meta_recv.at[0], sibling)
    meta_down = copy(cmeta.at[:, mine], meta(UP), meta_send.at[1], meta_recv.at[1], down)
    meta_up = copy(cmeta.at[:, mine], meta(LO), meta_send.at[2], meta_recv.at[2], up)
    meta_sib.start()
    pl.when(send_down)(meta_down.start)
    pl.when(send_up)(meta_up.start)
    for k in range(1, chunks):
        send(k)
    spread(core)

    def dots(row, col):
        return lax.dot_general(
            rows[pl.ds(row, n), :], rows[pl.ds(col, CH), :], (((1,), (1,)), ((), ())),
            preferred_element_type=jnp.float32,
        )

    def fold(values):
        return jnp.max(values.reshape(n // 8, 8, 128), axis=0)

    def lanes_of(col, h):
        return pl.ds(pl.multiple_of(col + h * 128, 128), 128)

    def pair(col, row):
        col, row = pl.multiple_of(col, CH), pl.multiple_of(row, n)
        dot = dots(row, col)
        at = pl.ds(row, n)
        scale, own_id, own_valid = rmeta[0, at, :], rmeta[1, at, :], rmeta[2, at, :]
        row_best = racc[at, :]
        for h in range(CH // 128):
            lane = lanes_of(col, h)
            d = dot[:, h * 128 : (h + 1) * 128]
            row_best = jnp.maximum(row_best, jnp.where(own_id == cmeta[2:3, lane], d * cmeta[0:1, lane], LOW))
            col_best = fold(jnp.where(own_valid == cmeta[1:2, lane], d * scale, LOW))
            cacc[:, lane] = jnp.maximum(cacc[:, lane], col_best)
        racc[at, :] = row_best

    def own_chunk(k, _):
        row = pl.multiple_of(core * n, n)
        col = pl.multiple_of(row + k * CH, CH)
        dot = dots(row, col)
        at = pl.ds(row, n)
        scale, own_valid = rmeta[0, at, :], rmeta[2, at, :]
        apart = lax.broadcasted_iota(jnp.int32, (n, 128), 0) - lax.broadcasted_iota(jnp.int32, (n, 128), 1)
        for h in range(CH // 128):
            lane = lanes_of(col, h)
            d = dot[:, h * 128 : (h + 1) * 128]
            keep = jnp.logical_and(own_valid == cmeta[1:2, lane], apart != k * CH + h * 128)
            cacc[:, lane] = fold(jnp.where(keep, d * scale, LOW))
        return 0

    lax.fori_loop(0, chunks, own_chunk, 0)

    meta_sib.wait_recv()
    theirs = pl.ds(pl.multiple_of(n - core * n, n), n)
    copy(emb, rows.at[theirs], sib_sem.at[0], sib_sem.at[1], sibling).wait_recv()
    spread(1 - core)

    def finish(slot):
        for t in range(n // 128):
            at = pl.ds(pl.multiple_of(slot * n + t * 128, 128), 128)
            best = jnp.max(cacc[:, at], axis=0, keepdims=True)
            if not (isinstance(slot, int) and slot == UP):
                best = jnp.maximum(best, jnp.max(racc[at, :].T, axis=0, keepdims=True))
            vec[slot, t : t + 1, :] = best * cmeta[0:1, at]

    send_vec_up = copy(vec.at[UP], got.at[1], vec_send.at[1], vec_recv.at[1], above)
    send_vec_lo = copy(vec.at[LO], got.at[2], vec_send.at[2], vec_recv.at[2], below)
    send_vec_sib = copy(vec.at[1 - core], got.at[0], vec_send.at[0], vec_recv.at[0], sibling)

    def stage(e, _):
        arrival = e >= 1
        k = jnp.maximum(e - 1, 0)
        k = jnp.where(first, k, lax.rem(k, 2) * half + k // 2)

        @pl.when(e == 1)
        def _():
            pl.when(has_up)(meta_down.wait_recv)
            pl.when(has_up)(lambda: spread(UP))
            pl.when(has_lo)(meta_up.wait_recv)
            pl.when(has_lo)(lambda: spread(LO))

            @pl.when(second)
            def _():
                ups[WAIT_B].wait_send()
                send_third()
                for j in range(half):
                    forward(j)

        @pl.when(jnp.logical_and(first, e == jnp.where(high, 2, STAGE_A)))
        def _():
            send_third()
            for j in range(half):
                forward(j)

        full = e == chunks

        def unit(j, _):
            newest = j >= chunks

            @pl.when(jnp.logical_and(jnp.logical_and(arrival, j == 0), has_lo))
            def _():
                copy(emb_part(k), rows.at[part(LO, k)], lo_send.at[k], lo_recv.at[k], up).wait_recv()

            @pl.when(jnp.logical_and(jnp.logical_and(arrival, j == chunks), has_up))
            def _():
                copy(emb_part(k), rows.at[part(UP, k)], up_send.at[k], up_recv.at[k], down).wait_recv()

            from_lo = jnp.logical_and(arrival, j == 0)
            slot = jnp.where(arrival, jnp.where(from_lo, LO, UP), B)
            chunk = jnp.where(arrival, jnp.where(jnp.logical_or(from_lo, newest), k, j - 1), j)
            row = jnp.where(
                arrival, jnp.where(from_lo, B, jnp.where(j > chunks, j - chunks - 1, LO)), A
            )
            crossing = jnp.logical_and(first, full)
            wanted = jnp.where(
                arrival,
                jnp.where(
                    from_lo,
                    jnp.logical_not(lo_down).astype(jnp.int32),
                    jnp.where(
                        j > chunks, has_up.astype(jnp.int32), crossing.astype(jnp.int32)
                    ),
                ),
                jnp.logical_and(second, j < chunks).astype(jnp.int32),
            )
            pl.when(wanted == 1)(lambda: pair(slot * n + chunk * CH, row * n))

            @pl.when(jnp.logical_and(jnp.logical_and(has_lo, full), j == chunks * (1 - core)))
            def _():
                finish(LO)
                send_vec_lo.start()

            return 0

        lax.fori_loop(0, chunks + 3, unit, 0)
        return 0

    lax.fori_loop(0, chunks + 1, stage, 0)

    @pl.when(has_up)
    def _():
        finish(UP)
        send_vec_up.start()

    finish(1 - core)
    send_vec_sib.start()
    finish(core)
    best = jnp.maximum(vec[core], -2.0)
    got_down, got_up = send_down, send_up
    send_vec_sib.wait_recv()
    best = jnp.maximum(best, got[0])
    out[...] = best

    @pl.when(got_down)
    def _():
        send_vec_up.wait_recv()
        out[...] = jnp.maximum(out[...], got[1])

    @pl.when(got_up)
    def _():
        send_vec_lo.wait_recv()
        out[...] = jnp.maximum(out[...], got[2])

    swap.wait_send()
    meta_sib.wait_send()
    send_vec_sib.wait_send()
    pl.when(send_down)(meta_down.wait_send)
    pl.when(send_up)(meta_up.wait_send)
    pl.when(has_up)(send_vec_up.wait_send)
    pl.when(has_lo)(send_vec_lo.wait_send)
    for k in range(half):
        pl.when(uses_via)(vias[k].wait_send)
        pl.when(is_relay)(fwd_up[k].wait_send)
    for k in range(chunks):
        pl.when(send_down if k < half else first)(downs[k].wait_send)
        if k == WAIT_B:
            if k < half:
                pl.when(via_up)(ups[k].wait_send)
        else:
            pl.when(send_up if k < half else second)(ups[k].wait_send)


def shards(blocks, embeddings, cluster_ids, valid_counts):
    n, d = embeddings.shape
    chunks = n // CH
    dma = pltpu.SemaphoreType.DMA
    best = pl.pallas_call(
        functools.partial(kernel, blocks),
        out_shape=jax.ShapeDtypeStruct((n // 128, 128), jnp.float32),
        in_specs=[
            pl.BlockSpec(memory_space=pl.ANY),
            pl.BlockSpec(memory_space=pltpu.VMEM),
            pl.BlockSpec(memory_space=pltpu.SMEM),
        ],
        out_specs=pl.BlockSpec(memory_space=pltpu.VMEM),
        scratch_shapes=[
            pltpu.VMEM((4 * n, d), jnp.bfloat16),
            pltpu.VMEM((n // 2, d), jnp.bfloat16),
            pltpu.VMEM((8, 4 * n), jnp.float32),
            pltpu.VMEM((3, 4 * n, 128), jnp.float32),
            pltpu.VMEM((4 * n, 128), jnp.float32),
            pltpu.VMEM((8, 4 * n), jnp.float32),
            pltpu.VMEM((4, n // 128, 128), jnp.float32),
            pltpu.VMEM((3, n // 128, 128), jnp.float32),
            dma(()), dma((2,)),
            dma((chunks,)), dma((chunks,)), dma((chunks,)), dma((chunks,)),
            dma((chunks // 2,)), dma((chunks // 2,)), dma((chunks // 2,)),
            dma((3,)), dma((3,)), dma((3,)), dma((3,)),
        ],
        compiler_params=pltpu.CompilerParams(
            collective_id=0, has_side_effects=True, vmem_limit_bytes=53 * 2**20
        ),
        name="neighbour_cosines",
    )(embeddings, cluster_ids.reshape(1, n), valid_counts)
    return best.reshape(n)


def solution(mesh):
    placed = (P(("grp", "mem"), None), P(("grp", "mem")), P(("grp", "mem")))
    return jax.shard_map(
        functools.partial(shards, mesh.size),
        mesh=mesh, in_specs=placed, out_specs=P(("grp", "mem")), check_vma=False,
    )
```
